256 devices in a mesh: segment: 8 (over z), ctx: 32 (over y, x, core).
Axes of the slice: x: 4, y: 4, z: 8, core: 2. Of those that a mesh axis runs over, the one named last changes fastest.
Arguments:
- acts: bfloat16 [8, 4096, 2048], P('segment', 'ctx'), may hold values from -10 to 10
- norm_gains: float32 [8, 3, 2048], P('segment'), may hold values from 0.25 to 1.75
- w_kv: bfloat16 [8, 2048, 1024], P('segment', None, 'ctx'), may hold values from -1 to 36.35534
- dt_in: bfloat16 [8, 2048, 128], P('segment'), may hold values from -0.125 to 0.125
- dt_out: bfloat16 [8, 128, 2048], P('segment'), may hold values from -0.5 to 0.5
- dt_bias: float32 [8, 2048], P('segment'), may hold values from -3 to -1
- decay_rate: float32 [8, 2048], P('segment'), may hold values from 0.002 to 2
- w_bc: bfloat16 [8, 2048, 32], P('segment'), may hold values from -0.03125 to 0.03125
- skip_gain: float32 [8, 2048], P('segment'), may hold values from 0.25 to 1.75
- w_router: bfloat16 [8, 2048, 4], P('segment'), may hold values from -1.109145 to 1.109145
- routes: int32 [8, 4096, 2], P('segment', 'ctx'), may hold values from 0 to 3, all different within a row; in each aligned block of 128 rows (0 to 127, 128 to 255, ..., all dimensions but the last counted through in order) at most 64 rows name the same one
- w_up: bfloat16 [8, 2048, 28672], P('segment', None, 'ctx'), may hold values from -0.125 to 0.125
- w_down: bfloat16 [8, 28672, 2048], P('segment', 'ctx'), may hold values from -0.0625 to 0.0625
Outputs:
- handed: bfloat16 [8, 4096, 2048], P('segment', 'ctx')
The draws below stay inside these ranges and needn't reach their ends.
Inputs may be any that keep to these rules, and one draw needn't show every extreme that they name: `routes`: in each section, the 128 rows of one context shard name every expert exactly 64 times; a token's 2 experts differ.
All inputs are finite; a program needn't handle non-finite values.
Results may differ from the reference program's by a relative error of at most 0.017.
Values may be sent and summed in bfloat16 or wider, within the bound.
A program may use at most 128 MiB of HBM per device.

```python
import math
import jax
import jax.numpy as jnp
import numpy as np
from jax import lax

D = 2048
HEADS = 16
KVH = 4
HD = 128
NS = 16
RANK = 128
EXPERTS = 4
EFF = 7168
TOP = 2
TOK_DEV = 128
SECTIONS = 8
SEQ = 4096
CAP = 64
N_SEGMENT = 8
N_CTX = 32


def draw_acts(key, part):
    jitter_key = jax.random.fold_in(key, 11)
    jitter = jax.random.normal(jitter_key, (SECTIONS, SEQ, D), jnp.float32)
    values = jnp.clip(jitter, -6.0, 6.0)
    return values.astype(jnp.bfloat16)


def draw_w_kv(key, part):
    weight_key = jax.random.fold_in(key, 17)
    entries = jnp.clip(jax.random.normal(weight_key, (SECTIONS, D, 2 * KVH * HD), jnp.float32), -6.0, 6.0) * D ** (-0.5)
    return entries.astype(jnp.bfloat16)


def draw_w_router(key, part):
    router_key = jax.random.fold_in(key, 23)
    entries = jnp.clip(jax.random.normal(router_key, (SECTIONS, D, EXPERTS), jnp.float32), -6.0, 6.0) * D ** (-0.5)
    return entries.astype(jnp.bfloat16)


def shard_levels(key, dims, cuts, least, high):
    level = 1.0
    for axis_at, shards_of in cuts:
        draws = jax.random.uniform(jax.random.fold_in(jax.random.fold_in(key, 6), axis_at), (shards_of,), jnp.float32, least / len(cuts), high / len(cuts))
        level = level * jnp.repeat(jnp.exp(draws), dims[axis_at] // shards_of).reshape((-1,) + (1,) * (len(dims) - 1 - axis_at))
    return level


def assign_block(key, own, number, rows, count, top, limit, slope):
    order = jax.random.permutation(key, count)
    heavy_load, common = shares(count, rows * top, limit, slope, True), shares(count, rows * top, limit, slope, False)
    places = jnp.arange(count)

    def named(tallies, offset_by):
        used = int((tallies > 0).sum())
        fixed = max(1, used // 4)
        moved = fixed + (places - fixed + offset_by * (used - fixed)) % max(1, count - fixed)
        return jnp.zeros((count,), jnp.int32).at[order[jnp.where(places < fixed, places, moved)]].set(jnp.asarray(tallies, jnp.int32))

    tallies = jnp.where(number % 4 == 0, named(heavy_load, number // 4), named(common, number - number // 4 - 1))
    mixed = jax.random.permutation(jax.random.fold_in(own, 3), count)
    giver, receiver = mixed[0:count // 2 * 2:2], mixed[1:count // 2 * 2:2]
    slack = jnp.minimum(tallies[giver] - 1, limit - tallies[receiver]) // 2
    slack = jnp.where((giver == order[0]) | (receiver == order[0]) | (tallies[receiver] == 0), 0, jnp.maximum(slack, 0))
    moved = jax.random.randint(jax.random.fold_in(own, 4), (count // 2,), 0, 1 << 20) % (slack + 1)
    tallies = tallies.at[giver].add(-moved).at[receiver].add(moved)
    items = jnp.searchsorted(jnp.cumsum(tallies), jnp.arange(rows * top), side="right").astype(jnp.int32)
    grid = items.reshape(top, rows).T
    grid = grid[jax.random.permutation(jax.random.fold_in(own, 1), rows)]
    offset_by = jax.random.randint(jax.random.fold_in(own, 2), (rows, 1), 0, top)
    return jnp.take_along_axis(grid, (jnp.arange(top)[None, :] + offset_by) % top, axis=1)


def shares(number_of, total, most, lean, full):
    weights = [(1 << 20) // math.isqrt(rank ** lean) + 1 for rank in range(1, number_of + 1)]
    largest = most if full else min(most, max(-(-total // number_of), total * weights[0] // sum(weights)))
    least = 1 if total - largest >= number_of - 1 else 0
    counts, spare = [largest] + [least] * (number_of - 1), total - largest - least * (number_of - 1)
    while spare > 0:
        candidates = [i for i in range(1, number_of) if counts[i] < largest] or [i for i in range(1, number_of) if counts[i] < most]
        whole, budget = sum([weights[i] for i in candidates]), spare
        for i in candidates:
            addition = min(most - counts[i], max(1, budget * weights[i] // whole), spare)
            counts[i] = counts[i] + addition
            spare = spare - addition
    return np.array(counts)


def bell_draw(own_key, shape, scale, bound, shards=(), kind=jnp.bfloat16):
    values = jax.random.normal(own_key, shape, jnp.float32) * scale
    if len(shards) > 0:
        values = shard_levels(own_key, shape, shards, -0.22, 0.18) * values
    return jnp.clip(values, min=-bound, max=bound).astype(kind)


def setup_inputs(seed: int = 0) -> dict:
    arg_keys = jax.random.split(jax.random.key(seed), 14)
    acts = draw_acts(jax.random.fold_in(arg_keys[13], 71), 0)
    norm_gains = jnp.clip(1.0 + 0.15 * jax.random.normal(arg_keys[1], (SECTIONS, 3, D), jnp.float32), 0.25, 1.75)
    w_kv = draw_w_kv(jax.random.fold_in(arg_keys[13], 71), 0)
    dt_in = bell_draw(arg_keys[3], (SECTIONS, D, RANK), D ** -0.5, 0.125, ((0, 8),))
    dt_out = bell_draw(arg_keys[4], (SECTIONS, RANK, D), RANK ** -0.5, 0.5, ((0, 8),))
    dt_bias = jnp.clip(-3.0 + 2.0 * jax.random.uniform(arg_keys[5], (SECTIONS, D), jnp.float32) ** shard_levels(arg_keys[5], (SECTIONS, D), ((0, 8),), -0.2, 0.2), -3.0, -1.0)
    decay_rate = jnp.clip(jnp.exp(math.log(2.0) - 6.9077552 * jax.random.uniform(arg_keys[6], (SECTIONS, D), jnp.float32) ** shard_levels(arg_keys[6], (SECTIONS, D), ((0, 8),), -0.2, 0.2)), 0.002, 2.0)
    w_bc = bell_draw(arg_keys[7], (SECTIONS, D, 2 * NS), (16 * D) ** -0.5, 0.03125, ((0, 8),))
    skip_gain = jnp.clip(1.0 + 0.15 * jax.random.normal(arg_keys[8], (SECTIONS, D), jnp.float32), 0.25, 1.75)
    w_router = draw_w_router(jax.random.fold_in(arg_keys[13], 71), 0)
    routes_keys = jax.random.split(jax.random.fold_in(arg_keys[10], 1), SECTIONS * SEQ // TOK_DEV)
    routes_turns = jax.random.permutation(jax.random.fold_in(arg_keys[10], 3), SECTIONS * SEQ // TOK_DEV)
    routes = jax.vmap(lambda own, number: assign_block(jax.random.fold_in(arg_keys[10], 2), own, number, TOK_DEV, EXPERTS, TOP, CAP, 0))(routes_keys, routes_turns).reshape((SECTIONS, SEQ, TOP))
    w_up = bell_draw(arg_keys[11], (SECTIONS, D, EXPERTS * EFF), D ** -0.5, 0.125, ((0, 8), (2, 32)))
    w_down = bell_draw(arg_keys[12], (SECTIONS, EXPERTS * EFF, D), EFF ** -0.5, 0.0625, ((0, 8), (1, 32)))
    return {"acts": acts, "norm_gains": norm_gains, "w_kv": w_kv, "dt_in": dt_in, "dt_out": dt_out, "dt_bias": dt_bias, "decay_rate": decay_rate, "w_bc": w_bc, "skip_gain": skip_gain, "w_router": w_router, "routes": routes, "w_up": w_up, "w_down": w_down}


def rms_norm(values, gain):
    return values * lax.rsqrt(lax.optimization_barrier(jnp.mean(values * values, -1, keepdims=True)) + 1e-06) * gain

def attend(normed, kv_rows):
    seq = normed.shape[0]
    group = HEADS // KVH
    keys = kv_rows[:, :KVH * HD].reshape(seq, KVH, HD).astype(jnp.float32)
    values = kv_rows[:, KVH * HD:].reshape(seq, KVH, HD).astype(jnp.float32)
    width = min(512, seq)
    queries = normed.reshape(seq // width, width, KVH, group, HD)
    starts = jnp.arange(seq // width, dtype=jnp.int32) * width
    key_pos = jnp.arange(seq, dtype=jnp.int32)

    def block(item):
        query_block, start = item
        scores = jnp.einsum('tgrd,sgd->tgrs', query_block.astype(jnp.float32), keys) * HD ** (-0.5)
        query_pos = start + jnp.arange(width, dtype=jnp.int32)
        allowed = (key_pos[None, :] <= query_pos[:, None])[:, None, None, :]
        scores = jnp.where(allowed, scores, -1e+30)
        largest = lax.optimization_barrier(jnp.max(scores, -1, keepdims=True))
        weights = jnp.where(allowed, jnp.exp(scores - largest), 0.0)
        total = lax.optimization_barrier(jnp.sum(weights, -1))
        rounded = lax.optimization_barrier(weights.astype(jnp.bfloat16)).astype(jnp.float32)
        mixed = jnp.einsum('tgrs,sgd->tgrd', rounded, values)
        return (mixed / total[..., None]).reshape(width, KVH * group * HD)
    return lax.map(block, (queries, starts)).reshape(seq, KVH * group * HD)

def reference(acts, norm_gains, w_kv, dt_in, dt_out, dt_bias, decay_rate, w_bc, skip_gain, w_router, routes, w_up, w_down):
    parts = N_CTX // EXPERTS
    part_width = EFF // parts
    per_expert = SEQ * TOP // EXPERTS
    results = []
    for section in range(N_SEGMENT):
        start_x = acts[section].astype(jnp.float32)
        normed = rms_norm(start_x, norm_gains[section, 0]).astype(jnp.bfloat16)
        kv_rows = jnp.dot(normed, w_kv[section], preferred_element_type=jnp.float32).astype(jnp.bfloat16)
        first = start_x + attend(normed, kv_rows)
        mixed_in = rms_norm(first, norm_gains[section, 1]).astype(jnp.bfloat16)
        low_rank = jnp.dot(mixed_in, dt_in[section], preferred_element_type=jnp.float32).astype(jnp.bfloat16)
        step_size = jax.nn.softplus(jnp.dot(low_rank, dt_out[section], preferred_element_type=jnp.float32) + dt_bias[section])
        keep = jnp.exp(-step_size * decay_rate[section])
        both = jnp.dot(mixed_in, w_bc[section], preferred_element_type=jnp.float32)
        b_part = both[:, :NS]
        c_part = both[:, NS:]
        driven = step_size * mixed_in.astype(jnp.float32)

        def advance(state, item):
            keep_row, drive_row, b_row, c_row = item
            state = keep_row[:, None] * state + drive_row[:, None] * b_row[None, :]
            return (state, lax.optimization_barrier(jnp.sum(state * c_row[None, :], -1)))
        state_zero = jnp.zeros((D, NS), jnp.float32)
        _, read_out = lax.scan(advance, state_zero, (keep, driven, b_part, c_part))
        second = first + read_out + skip_gain[section] * mixed_in.astype(jnp.float32)
        expert_in = rms_norm(second, norm_gains[section, 2]).astype(jnp.bfloat16)
        logits = jnp.dot(expert_in, w_router[section], preferred_element_type=jnp.float32)
        chosen = jnp.take_along_axis(logits, routes[section], 1)
        gates = jax.nn.softmax(chosen, -1)
        flat_route = routes[section].reshape(-1)
        flat_gate = gates.reshape(-1)
        moe_sum = jnp.zeros((SEQ, D), jnp.float32)
        for expert in range(EXPERTS):
            picked = jnp.nonzero(flat_route == expert, size=per_expert)[0].astype(jnp.int32)
            token_rows = (picked // TOP).astype(jnp.int32)
            rows = expert_in[token_rows]
            up_cols = w_up[section][:, expert * EFF:(expert + 1) * EFF]
            hidden = jax.nn.silu(jnp.dot(rows, up_cols, preferred_element_type=jnp.float32)).astype(jnp.bfloat16)
            expert_out = jnp.zeros((per_expert, D), jnp.float32)
            for part in range(parts):
                low = expert * EFF + part * part_width
                piece = jnp.dot(hidden[:, part * part_width:(part + 1) * part_width], w_down[section][low:low + part_width], preferred_element_type=jnp.float32)
                expert_out = expert_out + piece.astype(jnp.bfloat16).astype(jnp.float32)
            moe_sum = moe_sum.at[token_rows].add(expert_out * flat_gate[picked][:, None])
        results.append((second + moe_sum).astype(jnp.bfloat16))
    return jnp.roll(jnp.stack(results), 1, 0)
```

```python
import functools

import jax
import jax.numpy as jnp
from jax import lax
from jax.experimental import pallas as pl
from jax.experimental.pallas import tpu as pltpu
from jax.sharding import PartitionSpec as P

HEADS = 16
KVH = 4
HD = 128
EXPERTS = 4


def entering(array, axis, join, neutral):
    place = lax.axis_index(axis)
    gathered = jax.tree.map(
        lambda a, kind: lax.all_gather(a.astype(kind), axis), array, (jnp.bfloat16, jnp.bfloat16)
    )
    state = jax.tree.map(lambda a, e: jnp.zeros_like(a) + jnp.asarray(e, a.dtype), array, neutral)

    def one(turn, state):
        return join(
            state,
            jax.tree.map(
                lambda a, own: lax.dynamic_index_in_dim(a, turn, 0, False).astype(own.dtype),
                gathered,
                array,
            ),
        )

    return lax.fori_loop(0, place, one, state)


def shifted(value, axis, steps):
    count = lax.axis_size(axis)
    pairs = [(source, (source + steps) % count) for source in range(count)]
    return lax.ppermute(value, axis, pairs)


def rms_norm(values, gain):
    return values * lax.rsqrt(jnp.mean(values * values, -1, keepdims=True) + 1e-06) * gain


def combine_states(earlier, later):
    return (earlier[0] * later[0], later[0][:, None] * earlier[1] + later[1])


X_CHIPS = 4
Y_CHIPS = 4
MIB = 1 << 20


def place(y, x, core):
    return {"ctx": (y * X_CHIPS + x) * 2 + core}


def coordinates():
    ctx = lax.axis_index("ctx")
    return lax.div(ctx, 2 * X_CHIPS), lax.rem(lax.div(ctx, 2), X_CHIPS), lax.rem(ctx, 2)


def greet(peers):
    barrier = pltpu.get_barrier_semaphore()
    for peer in peers:
        pl.semaphore_signal(barrier, inc=1, device_id=peer, device_id_type=pl.DeviceIdType.MESH)
    pl.semaphore_wait(barrier, len(peers))


def moe_kernel(
    packed,
    up_any,
    down_any,
    out,
    rows,
    parts,
    sibling_parts,
    far_parts,
    side_parts,
    up,
    down,
    hidden,
    weight_sem,
    send_y,
    recv_y,
    send_side,
    recv_side,
    send_far,
    recv_far,
    send_core,
    recv_core,
    back_core_send,
    back_core_recv,
    back_far_send,
    back_far_recv,
    back_side_send,
    back_side_recv,
    back_y_send,
    back_y_recv,
):
    y, x, core = coordinates()
    left = lax.rem(x + X_CHIPS - 1, X_CHIPS)
    right = lax.rem(x + 1, X_CHIPS)
    far = lax.rem(x + 2, X_CHIPS)
    chips = (x, left, right, far)
    on_left, on_right, on_core = place(y, left, core), place(y, right, core), place(y, x, 1 - core)
    started = []

    def row_of(k):
        return lax.rem(y + k, Y_CHIPS)

    def send(src, dst, send_sem, recv_sem, to):
        copy = pltpu.make_async_remote_copy(
            src_ref=src,
            dst_ref=dst,
            send_sem=send_sem,
            recv_sem=recv_sem,
            device_id=to,
            device_id_type=pl.DeviceIdType.MESH,
        )
        copy.start()
        started.append(copy)

    def arrived(dst, sem):
        pltpu.make_async_copy(dst, dst, sem).wait()

    load_up = pltpu.make_async_copy(up_any, up, weight_sem.at[0])
    load_down = pltpu.make_async_copy(down_any, down, weight_sem.at[1])
    load_up.start()
    load_down.start()
    greet([on_left, on_right, on_core] + [place(row_of(k), x, core) for k in (1, 2, 3)])

    def block(at, k):
        return rows.at[chips[at], core, row_of(k)]

    def own_block(k):
        send(block(0, k), block(0, k), send_side.at[0, k], recv_side.at[0, k], on_right)
        send(block(0, k), block(0, k), send_side.at[1, k], recv_side.at[1, k], on_left)
        send(block(0, k), block(0, k), send_core.at[0, k], recv_core.at[0, k], on_core)

    def side_block(k):
        arrived(block(1, k), recv_side.at[0, k])
        if k in (0, 1):
            send(block(1, k), block(1, k), send_far.at[k], recv_far.at[k], on_right)
        send(block(1, k), block(1, k), send_core.at[1, k], recv_core.at[1, k], on_core)
        arrived(block(2, k), recv_side.at[1, k])
        if k in (2, 3):
            send(block(2, k), block(2, k), send_far.at[k], recv_far.at[k], on_left)
        send(block(2, k), block(2, k), send_core.at[2, k], recv_core.at[2, k], on_core)

    def far_block(k):
        arrived(block(3, k), recv_far.at[k])
        send(block(3, k), block(3, k), send_core.at[3, k], recv_core.at[3, k], on_core)

    def from_core(at):
        for k in range(Y_CHIPS):
            other = rows.at[chips[at], 1 - core, row_of(k)]
            arrived(other, recv_core.at[at, k])

    def experts(at):
        chip = chips[at]

        def one_core(turn, carry):
            which = lax.rem(1 - core + turn, 2)
            taken = rows[chip, which].reshape(-1, rows.shape[-1])
            lifted = jnp.dot(taken, up[...], preferred_element_type=jnp.float32)
            hidden[...] = jax.nn.silu(lifted).astype(jnp.bfloat16)

            def columns(j, carry):
                span = pl.ds(pl.multiple_of(j * 512, 512), 512)
                lowered = jnp.dot(hidden[...], down[:, span], preferred_element_type=jnp.float32)
                parts[chip, which, :, :, span] = lowered.astype(jnp.bfloat16).reshape(
                    Y_CHIPS, -1, 512
                )
                return carry

            return lax.fori_loop(0, rows.shape[-1] // 512, columns, carry)

        lax.fori_loop(0, 2, one_core, 0)
        send(
            parts.at[chip, 1 - core],
            sibling_parts.at[chip],
            back_core_send.at[at],
            back_core_recv.at[at],
            on_core,
        )

    def added(*refs):
        total = refs[0][...].astype(jnp.float32)
        for ref in refs[1:]:
            total = total + ref[...].astype(jnp.float32)
        return total.astype(jnp.bfloat16)

    def mine(at, k):
        return parts.at[chips[at], core, row_of(k)]

    def theirs(at, k):
        return sibling_parts.at[chips[at], row_of(k)]

    for k in (1, 3, 2):
        send(
            packed.at[row_of(k)],
            rows.at[x, core, y],
            send_y.at[k],
            recv_y.at[4 - k],
            place(row_of(k), x, core),
        )
    rows[x, core, y] = packed[y]
    own_block(0)
    for k in (1, 3, 2):
        arrived(block(0, k), recv_y.at[k])
        own_block(k)
    load_up.wait()
    load_down.wait()
    from_core(0)
    side_block(0)
    experts(0)
    for k in (1, 3, 2):
        side_block(k)
    from_core(1)
    experts(1)
    far_block(0)
    from_core(2)
    experts(2)
    for k in (1, 3, 2):
        far_block(k)

    def core_sum(at):
        arrived(sibling_parts.at[chips[at]], back_core_recv.at[at])

    def to_side(at, k, relayed):
        if relayed:
            slot = far_parts.at[k]
            arrived(slot, back_far_recv.at[k])
            mine(at, k)[...] = added(mine(at, k), theirs(at, k), slot)
        else:
            mine(at, k)[...] = added(mine(at, k), theirs(at, k))
        to = on_left if at == 1 else on_right
        send(
            mine(at, k),
            side_parts.at[at - 1, k],
            back_side_send.at[at - 1, k],
            back_side_recv.at[at - 1, k],
            to,
        )

    core_sum(1)
    core_sum(2)
    for k in (3, 0):
        to_side(1, k, False)
    for k in (2, 1):
        to_side(2, k, False)
    from_core(3)
    experts(3)
    core_sum(3)
    for k in (2, 3, 1, 0):
        mine(3, k)[...] = added(mine(3, k), theirs(3, k))
        to = on_left if k in (2, 1) else on_right
        send(mine(3, k), far_parts.at[k], back_far_send.at[k], back_far_recv.at[k], to)
    core_sum(0)
    for k in (2, 3, 1, 0):
        to_side(1 if k in (2, 1) else 2, k, True)
    for k in (2, 3, 1, 0):
        for at in (1, 2):
            arrived(side_parts.at[at - 1, k], back_side_recv.at[at - 1, k])
        total = added(mine(0, k), theirs(0, k), side_parts.at[0, k], side_parts.at[1, k])
        if k == 0:
            out[y] = total
        else:
            mine(0, k)[...] = total
            send(
                mine(0, k),
                out.at[y],
                back_y_send.at[k],
                back_y_recv.at[4 - k],
                place(row_of(k), x, core),
            )
    for k in (1, 3, 2):
        arrived(out.at[row_of(k)], back_y_recv.at[k])
    for copy in started:
        copy.wait_send()


def mixture(packed, w_up, w_down):
    experts, capacity, width = packed.shape
    units = w_up.shape[1]
    kind = jnp.bfloat16
    block = (capacity, width)
    dma = pltpu.SemaphoreType.DMA
    return pl.pallas_call(
        moe_kernel,
        out_shape=jax.ShapeDtypeStruct(packed.shape, kind),
        in_specs=[
            pl.BlockSpec(memory_space=pltpu.VMEM),
            pl.BlockSpec(memory_space=pl.ANY),
            pl.BlockSpec(memory_space=pl.ANY),
        ],
        out_specs=pl.BlockSpec(memory_space=pltpu.VMEM),
        scratch_shapes=[
            pltpu.VMEM((X_CHIPS, 2, Y_CHIPS) + block, kind),
            pltpu.VMEM((X_CHIPS, 2, Y_CHIPS) + block, kind),
            pltpu.VMEM((X_CHIPS, Y_CHIPS) + block, kind),
            pltpu.VMEM((Y_CHIPS,) + block, kind),
            pltpu.VMEM((2, Y_CHIPS) + block, kind),
            pltpu.VMEM(w_up.shape, kind),
            pltpu.VMEM(w_down.shape, kind),
            pltpu.VMEM((Y_CHIPS * capacity, units), kind),
            dma((2,)),
            dma((4,)),
            dma((4,)),
            dma((2, 4)),
            dma((2, 4)),
            dma((4,)),
            dma((4,)),
            dma((4, 4)),
            dma((4, 4)),
            dma((4,)),
            dma((4,)),
            dma((4,)),
            dma((4,)),
            dma((2, 4)),
            dma((2, 4)),
            dma((4,)),
            dma((4,)),
        ],
        compiler_params=pltpu.CompilerParams(
            collective_id=1, has_side_effects=True, vmem_limit_bytes=56 * MIB
        ),
        name="mixture",
    )(packed, w_up, w_down)


def on_device(
    acts,
    norm_gains,
    w_kv,
    dt_in,
    dt_out,
    dt_bias,
    decay_rate,
    w_bc,
    skip_gain,
    w_router,
    routes,
    w_up,
    w_down,
):
    shard_index = lax.axis_index("ctx")
    start_x = acts[0].astype(jnp.float32)
    rows_here = start_x.shape[0]
    width = start_x.shape[1]
    group = HEADS // KVH
    normed = rms_norm(start_x, norm_gains[0, 0]).astype(jnp.bfloat16)
    kv_rows = jnp.dot(
        normed,
        lax.all_gather(w_kv[0], "ctx", axis=1, tiled=True),
        preferred_element_type=jnp.float32,
    ).astype(jnp.bfloat16)
    keys = kv_rows[:, : KVH * HD].reshape(rows_here, KVH, HD)
    values = kv_rows[:, KVH * HD :].reshape(rows_here, KVH, HD)
    queries = normed.reshape(rows_here, KVH, group, HD)
    query_pos = shard_index * rows_here + jnp.arange(rows_here, dtype=jnp.int32)
    running = jnp.full((rows_here, KVH, group), -1e30, jnp.float32)
    key_piece = lax.all_gather(keys, "ctx", axis=0, tiled=True)
    value_piece = lax.all_gather(values, "ctx", axis=0, tiled=True)
    key_pos = jnp.arange(key_piece.shape[0], dtype=jnp.int32)
    scores = jnp.einsum(
        "tgrd,sgd->tgrs", queries, key_piece, preferred_element_type=jnp.float32
    ) * HD ** (-0.5)
    allowed = (key_pos[None, :] <= query_pos[:, None])[:, None, None, :]
    scores = jnp.where(allowed, scores, -1e30)
    newest = jnp.maximum(running, jnp.max(scores, -1))
    weights = jnp.where(allowed, jnp.exp(scores - newest[..., None]), 0.0)
    total = jnp.sum(weights, -1)
    summed = jnp.einsum(
        "tgrs,sgd->tgrd",
        weights.astype(jnp.bfloat16),
        value_piece,
        preferred_element_type=jnp.float32,
    )
    _, total, summed = (newest, total, summed)
    first = start_x + (summed / total[..., None]).reshape(rows_here, width)
    mixed_in = rms_norm(first, norm_gains[0, 1]).astype(jnp.bfloat16)
    low_rank = jnp.dot(mixed_in, dt_in[0], preferred_element_type=jnp.float32).astype(jnp.bfloat16)
    step_size = jax.nn.softplus(
        jnp.dot(low_rank, dt_out[0], preferred_element_type=jnp.float32) + dt_bias[0]
    )
    log_decay = step_size * decay_rate[0]
    state_width = w_bc.shape[2] // 2
    both = jnp.dot(mixed_in, w_bc[0], preferred_element_type=jnp.float32)
    b_part = both[:, :state_width]
    c_part = both[:, state_width:]
    driven = step_size * mixed_in.astype(jnp.float32)
    block_rows = min(32, rows_here)
    block_count = rows_here // block_rows
    lower_mask = jnp.arange(block_rows)[:, None] >= jnp.arange(block_rows)[None, :]
    lower_float = lower_mask.astype(jnp.float32)

    def block_scan(carry, item):
        state, offset_sum = carry
        rate_block, drive_block, b_block, c_block = item
        running_sum = jnp.dot(lower_float, rate_block, precision=lax.Precision.HIGHEST)
        coupling = jnp.dot(c_block, b_block.T, precision=lax.Precision.HIGHEST)
        distance = jnp.maximum(running_sum[:, None, :] - running_sum[None, :, :], 0.0)
        fading = jnp.where(lower_mask[:, :, None], jnp.exp(-distance), 0.0)
        within = jnp.sum(fading * coupling[:, :, None] * drive_block[None, :, :], 1)
        decay_in = jnp.exp(-running_sum)
        from_state = jnp.dot(c_block, state.T, precision=lax.Precision.HIGHEST) * decay_in
        tail_weight = jnp.exp(running_sum - running_sum[-1][None, :]) * drive_block
        state = decay_in[-1][:, None] * state + jnp.dot(
            tail_weight.T, b_block, precision=lax.Precision.HIGHEST
        )
        shard_decay = jnp.exp(-(offset_sum[None, :] + running_sum))
        return ((state, offset_sum + running_sum[-1]), (within + from_state, shard_decay))

    start_carry = (jnp.zeros((width, state_width), jnp.float32), jnp.zeros((width,), jnp.float32))
    scan_items = (
        log_decay.reshape(block_count, block_rows, width),
        driven.reshape(block_count, block_rows, width),
        b_part.reshape(block_count, block_rows, state_width),
        c_part.reshape(block_count, block_rows, state_width),
    )
    (end_state, end_offset), (block_out, block_decay) = lax.scan(
        block_scan, start_carry, scan_items
    )
    local_out = block_out.reshape(rows_here, width)
    products = block_decay.reshape(rows_here, width)
    end_product = jnp.exp(-end_offset)
    identity = (jnp.ones((width,), jnp.float32), jnp.zeros((width, state_width), jnp.float32))
    incoming = entering((end_product, end_state), "ctx", combine_states, identity)[1]
    carried = jnp.dot(c_part, incoming.T, precision=lax.Precision.HIGHEST) * products
    second = first + local_out + carried + skip_gain[0] * mixed_in.astype(jnp.float32)
    expert_in = rms_norm(second, norm_gains[0, 2]).astype(jnp.bfloat16)
    logits = jnp.dot(expert_in, w_router[0], preferred_element_type=jnp.float32)
    top_count = routes.shape[2]
    expert_ids = jnp.arange(EXPERTS, dtype=jnp.int32)
    picked = (routes[0][:, :, None] == expert_ids[None, None, :]).astype(jnp.float32)
    chosen = jnp.sum(picked * logits[:, None, :], -1)
    gates = jax.nn.softmax(chosen, -1)
    flat_route = routes[0].reshape(-1)
    flat_hits = (flat_route[:, None] == expert_ids[None, :]).astype(jnp.int32)
    earlier_hits = jnp.cumsum(flat_hits, 0) - flat_hits
    slot_rank = jnp.sum(earlier_hits * flat_hits, -1)
    capacity = rows_here * top_count // EXPERTS
    position = flat_route * capacity + slot_rank
    slot_ids = jnp.arange(EXPERTS * capacity, dtype=jnp.int32)
    placing = (position[None, :] == slot_ids[:, None]).astype(jnp.bfloat16)
    repeated = jnp.repeat(expert_in, top_count, 0)
    packed = (
        jnp.dot(placing, repeated, preferred_element_type=jnp.float32)
        .astype(jnp.bfloat16)
        .reshape(EXPERTS, capacity, width)
    )
    expert_out = (
        mixture(packed, w_up[0], w_down[0])
        .astype(jnp.float32)
        .reshape(EXPERTS * capacity, width)
    )
    weighting = (position[:, None] == slot_ids[None, :]).astype(jnp.float32) * gates.reshape(-1)[
        :, None
    ]
    moe_rows = (
        jnp.dot(weighting, expert_out, precision=lax.Precision.HIGHEST)
        .reshape(rows_here, top_count, width)
        .sum(1)
    )
    finished = (second + moe_rows).astype(jnp.bfloat16)
    return shifted(finished[None], "segment", 1)


def solution(mesh):
    in_specs = (
        P("segment", "ctx", None),
        P("segment", None, None),
        P("segment", None, "ctx"),
        P("segment", None, None),
        P("segment", None, None),
        P("segment", None),
        P("segment", None),
        P("segment", None, None),
        P("segment", None),
        P("segment", None, None),
        P("segment", "ctx", None),
        P("segment", None, "ctx"),
        P("segment", "ctx", None),
    )
    out_specs = P("segment", "ctx", None)
    return jax.shard_map(
        on_device, mesh=mesh, in_specs=in_specs, out_specs=out_specs, check_vma=False
    )
```

```python
import jax
import jax.numpy as jnp
from jax import lax
from jax.experimental import pallas as pl
from jax.experimental.pallas import tpu as pltpu
from jax.sharding import PartitionSpec as P

HEADS = 16
KVH = 4
HD = 128
EXPERTS = 4
X_CHIPS = 4
Y_CHIPS = 4
MIB = 1 << 20
LOG2E = 1.4426950408889634


def place(y, x, core):
    return {"ctx": (y * X_CHIPS + x) * 2 + core}


def coordinates():
    ctx = lax.axis_index("ctx")
    return lax.div(ctx, 2 * X_CHIPS), lax.rem(lax.div(ctx, 2), X_CHIPS), lax.rem(ctx, 2)


def greet(peers):
    barrier = pltpu.get_barrier_semaphore()
    for peer in peers:
        pl.semaphore_signal(barrier, inc=1, device_id=peer, device_id_type=pl.DeviceIdType.MESH)


def greeted(count):
    pl.semaphore_wait(pltpu.get_barrier_semaphore(), count)


def arrived(dst, sem):
    pltpu.make_async_copy(dst, dst, sem).wait()


def rms_norm(values, gain):
    return values * lax.rsqrt(jnp.mean(values * values, -1, keepdims=True) + 1e-06) * gain


class Sender:
    def __init__(self):
        self.started = []

    def __call__(self, src, dst, send_sem, recv_sem, to):
        copy = pltpu.make_async_remote_copy(
            src_ref=src,
            dst_ref=dst,
            send_sem=send_sem,
            recv_sem=recv_sem,
            device_id=to,
            device_id_type=pl.DeviceIdType.MESH,
        )
        copy.start()
        self.started.append(copy)

    def finish(self):
        for copy in self.started:
            copy.wait_send()


class Gather:
    def __init__(self, buf, sems, send):
        self.buf, self.send = buf, send
        self.s1, self.r1, self.s2, self.r2, self.sc, self.rc = sems
        self.y, self.x, self.core = coordinates()

    def near(self, half, step, first):
        along_x = (half == 0) == first
        if along_x:
            return place(self.y, lax.rem(self.x + step, X_CHIPS), self.core)
        return place(lax.rem(self.y + step, Y_CHIPS), self.x, self.core)

    def block(self, half, step):
        if half == 0:
            return self.buf.at[self.y, lax.rem(self.x + step, X_CHIPS), self.core, 0]
        return self.buf.at[lax.rem(self.y + step, Y_CHIPS), self.x, self.core, 1]

    def line(self, half, step, pair=None, other=False):
        span = slice(None) if pair is None else pl.ds(2 * pair, 2)
        core = 1 - self.core if other else self.core
        if half == 0:
            return self.buf.at[lax.rem(self.y + step, Y_CHIPS), span, core, 0]
        return self.buf.at[span, lax.rem(self.x + step, X_CHIPS), core, 1]

    def both_ways(self, ref, half, first, s, r):
        self.send(ref, ref, s(0), r(0), self.near(half, 1, first))
        self.send(ref, ref, s(1), r(1), self.near(half, 3, first))

    def start(self, half):
        s, r = (lambda i: self.s1.at[half, i]), (lambda i: self.r1.at[half, i])
        self.both_ways(self.block(half, 0), half, True, s, r)

    def relay(self, half):
        ref = self.block(half, 3 + 2 * self.core)
        arrived(ref, self.r1.at[half, self.core])
        to = self.near(half, 1 + 2 * self.core, True)
        self.send(ref, ref, self.s1.at[half, 2], self.r1.at[half, 2], to)

    def turn(self, half):
        arrived(self.block(half, 1 + 2 * self.core), self.r1.at[half, 1 - self.core])
        arrived(self.block(half, 2), self.r1.at[half, 2])
        for pair in range(2):
            s, r = (lambda i: self.s2.at[half, pair, i]), (lambda i: self.r2.at[half, pair, i])
            self.both_ways(self.line(half, 0, pair), half, False, s, r)
        self.share(half, 0)

    def share(self, half, step):
        ref = self.line(half, step)
        to = place(self.y, self.x, 1 - self.core)
        self.send(ref, ref, self.sc.at[half, step], self.rc.at[half, step], to)

    def relay_line(self, half, pair):
        ref = self.line(half, 3 + 2 * self.core, pair)
        arrived(ref, self.r2.at[half, pair, self.core])
        to = self.near(half, 1 + 2 * self.core, False)
        self.send(ref, ref, self.s2.at[half, pair, 2], self.r2.at[half, pair, 2], to)

    def sides(self, half):
        for pair in range(2):
            ref = self.line(half, 1 + 2 * self.core, pair)
            arrived(ref, self.r2.at[half, pair, 1 - self.core])
        self.share(half, 3)
        self.share(half, 1)

    def far(self, half):
        for pair in range(2):
            arrived(self.line(half, 2, pair), self.r2.at[half, pair, 2])
        self.share(half, 2)

    def shared(self, half, step):
        arrived(self.line(half, step, other=True), self.rc.at[half, step])


def mixer_kernel(
    acts,
    gains,
    w_kv,
    dt_in_any,
    dt_out_any,
    dt_bias,
    decay_rate,
    w_bc_any,
    skip_gain,
    w_router_any,
    routes,
    packed,
    weighting,
    second,
    weights,
    kv,
    normed,
    queries,
    largest,
    total,
    summed,
    first,
    mixed,
    keep,
    drive,
    both_vmem,
    both,
    message,
    inbox,
    outbox,
    incoming,
    dt_in,
    dt_out,
    w_bc,
    w_router,
    load_sem,
    scan_send,
    scan_recv,
    w_s1,
    w_r1,
    w_s2,
    w_r2,
    w_sc,
    w_rc,
    kv_s1,
    kv_r1,
    kv_s2,
    kv_r2,
    kv_sc,
    kv_rc,
):
    y, x, core = coordinates()
    ctx = lax.axis_index("ctx")
    devices = 2 * X_CHIPS * Y_CHIPS
    rows, width = acts.shape
    lanes = 128
    blocks = width // lanes
    f32, bf16 = jnp.float32, jnp.bfloat16
    loads = [
        pltpu.make_async_copy(src, dst, load_sem.at[i])
        for i, (src, dst) in enumerate(
            [(dt_in_any, dt_in), (dt_out_any, dt_out), (w_bc_any, w_bc), (w_router_any, w_router)]
        )
    ]
    for load in loads:
        load.start()
    barrier = pltpu.get_barrier_semaphore()

    def hail(step, carry):
        peer = {"ctx": lax.rem(ctx + step, devices)}
        pl.semaphore_signal(barrier, inc=1, device_id=peer, device_id_type=pl.DeviceIdType.MESH)
        return carry

    lax.fori_loop(1, devices, hail, 0)
    send = Sender()

    for half in range(2):
        weights[y, x, core, half] = w_kv[half * 16 : half * 16 + 16]
    normed[...] = rms_norm(acts[...].astype(f32), gains[0:1]).astype(bf16)
    for head in range(HEADS):
        group, place_in = divmod(head, HEADS // KVH)
        queries[group, place_in * rows : (place_in + 1) * rows] = normed[:, head * HD : (head + 1) * HD]
    pl.semaphore_wait(barrier, devices - 1)
    w_gather = Gather(weights, (w_s1, w_r1, w_s2, w_r2, w_sc, w_rc), send)
    for step in (w_gather.start, w_gather.relay, w_gather.turn):
        for half in range(2):
            step(half)
    for pair in range(2):
        for half in range(2):
            w_gather.relay_line(half, pair)
    for step in (w_gather.sides, w_gather.far):
        for half in range(2):
            step(half)
    for half in range(2):
        for step in range(4):
            w_gather.shared(half, step)

    for part in range(4):
        made = lax.dot_general(
            normed[...],
            weights[part].reshape(2 * HD, width),
            (((1,), (1,)), ((), ())),
            preferred_element_type=f32,
        ).astype(bf16)
        for head in range(2):
            kv[y, x, core, part % 2, part // 2 * 2 + head] = made[:, head * HD : (head + 1) * HD]

    kv_gather = Gather(kv, (kv_s1, kv_r1, kv_s2, kv_r2, kv_sc, kv_rc), send)
    for step in (kv_gather.start, kv_gather.relay, kv_gather.turn):
        for half in range(2):
            step(half)
    group = HEADS // KVH
    keys_here = 2 * X_CHIPS * rows
    queue = lax.broadcasted_iota(jnp.int32, (group, rows, 1), 1).reshape(group * rows, 1) + ctx * rows
    column = lax.broadcasted_iota(jnp.int32, (1, keys_here), 1)

    def attend(half, step):
        kv_gather.shared(half, step)
        if half == 0:
            line = lax.rem(y + step, Y_CHIPS)
            key_pos = column + line * keys_here
        else:
            line = lax.rem(x + step, X_CHIPS)
            per_chip = 2 * rows
            key_pos = column // per_chip * keys_here + line * per_chip + column % per_chip
        allowed = key_pos <= queue

        def one_head(head, carry):
            g = 2 * half + head
            if half == 0:
                k, v = kv[line, :, :, 0, head], kv[line, :, :, 0, 2 + head]
            else:
                k, v = kv[:, line, :, 1, head], kv[:, line, :, 1, 2 + head]
            k, v = k.reshape(keys_here, HD), v.reshape(keys_here, HD)
            scores = lax.dot_general(
                queries[g], k, (((1,), (1,)), ((), ())), preferred_element_type=f32
            ) * (HD**-0.5 * LOG2E)
            scores = jnp.where(allowed, scores, -1e30)
            top = jnp.max(scores, -1, keepdims=True)
            if step == 0:
                newest = jnp.broadcast_to(top, (group * rows, lanes))
            else:
                newest = jnp.maximum(largest[g], top)
            wide = jnp.concatenate([newest] * (keys_here // lanes), 1)
            probs = jnp.exp2(scores - wide)
            sums = jnp.sum(probs, -1, keepdims=True)
            mixed_in = jnp.dot(probs.astype(bf16), v, preferred_element_type=f32)
            if step == 0:
                total[g] = jnp.broadcast_to(sums, (group * rows, lanes))
                summed[g] = mixed_in
            else:
                fade = jnp.exp2(largest[g] - newest)
                total[g] = total[g] * fade + sums
                summed[g] = summed[g] * fade + mixed_in
            largest[g] = newest
            return carry

        lax.fori_loop(0, 2, one_head, 0)

    for half in range(2):
        attend(half, 0)
    for pair in range(2):
        for half in range(2):
            kv_gather.relay_line(half, pair)
    for half in range(2):
        kv_gather.sides(half)
    for half in range(2):
        for step in (3, 1):
            attend(half, step)
    for half in range(2):
        kv_gather.far(half)
    for half in range(2):
        attend(half, 2)

    for head in range(HEADS):
        g, r = divmod(head, group)
        span = slice(head * HD, (head + 1) * HD)
        here = slice(r * rows, (r + 1) * rows)
        first[:, span] = acts[:, span].astype(f32) + summed[g, here] / total[g, here]

    mixed[...] = rms_norm(first[...], gains[1:2]).astype(bf16)
    for load in loads:
        load.wait()
    both_vmem[:, 0:32] = jnp.dot(mixed[...], w_bc[...], preferred_element_type=f32)
    to_scalars = pltpu.make_async_copy(both_vmem, both, load_sem.at[0])
    to_scalars.start()
    low_rank = jnp.dot(mixed[...], dt_in[...], preferred_element_type=f32).astype(bf16)
    for i in range(blocks):
        span = slice(i * lanes, (i + 1) * lanes)
        raw = jnp.dot(low_rank, dt_out[:, span], preferred_element_type=f32) + dt_bias[:, span]
        step_size = jnp.maximum(raw, 0.0) + jnp.log1p(jnp.exp(-jnp.abs(raw)))
        keep[:, i, :] = jnp.exp(-step_size * decay_rate[:, span])
        drive[:, i, :] = step_size * mixed[:, span].astype(f32)
    to_scalars.wait()
    states = 16

    def advance(t, carry):
        state, product = carry
        kept, driven = keep[t], drive[t]
        state = tuple(s * kept + driven * both[t, n] for n, s in enumerate(state))
        terms = [s * both[t, states + n] for n, s in enumerate(state)]
        while len(terms) > 1:
            terms = [a + b for a, b in zip(terms[::2], terms[1::2])]
        product = product * kept
        drive[t] = terms[0]
        keep[t] = product
        return state, product

    zero = jnp.zeros((blocks, lanes), f32)
    state, product = lax.fori_loop(
        0, rows, advance, ((zero,) * states, jnp.ones((blocks, lanes), f32))
    )

    for n in range(states):
        for part in range(2):
            message[2 * n + part, 0] = state[n][part * 8 : part * 8 + 8]
            message[2 * n + part, 1] = product[part * 8 : part * 8 + 8]

    def swap(count, mine, theirs, semaphore):
        own = pltpu.make_async_copy(mine(ctx), theirs(ctx), scan_recv.at[semaphore])
        own.start()

        def one(step, carry):
            peer = lax.rem(ctx + step, devices)
            pltpu.make_async_remote_copy(
                src_ref=mine(peer),
                dst_ref=theirs(ctx),
                send_sem=scan_send.at[semaphore],
                recv_sem=scan_recv.at[semaphore],
                device_id={"ctx": peer},
                device_id_type=pl.DeviceIdType.MESH,
            ).start()
            return carry

        lax.fori_loop(1, devices, one, 0)

    swap(0, lambda j: message.at[j], lambda j: inbox.at[j], 0)
    arrived(inbox, scan_recv.at[0])

    def join(turn, entering):
        outbox[turn] = entering
        return inbox[turn, 1] * entering + inbox[turn, 0]

    lax.fori_loop(0, devices, join, jnp.zeros((8, lanes), f32))

    def slot(j):
        return incoming.at[lax.div(j, 2), pl.ds(pl.multiple_of(lax.rem(j, 2) * 8, 8), 8)]

    swap(0, lambda j: outbox.at[j], slot, 1)
    arrived(incoming, scan_recv.at[1])

    def carry_in(t, held):
        terms = [s * both[t, states + n] for n, s in enumerate(held)]
        while len(terms) > 1:
            terms = [a + b for a, b in zip(terms[::2], terms[1::2])]
        drive[t] = drive[t] + keep[t] * terms[0]
        return held

    lax.fori_loop(0, rows, carry_in, tuple(incoming[n] for n in range(states)))
    for i in range(blocks):
        span = slice(i * lanes, (i + 1) * lanes)
        second[:, span] = (
            first[:, span] + drive[:, i, :] + skip_gain[:, span] * mixed[:, span].astype(f32)
        )

    normed[...] = rms_norm(second[...], gains[2:3]).astype(bf16)
    logits = jnp.dot(normed[...], w_router[...], preferred_element_type=f32)
    expert = lax.broadcasted_iota(jnp.int32, (rows, EXPERTS), 1)
    hits = [(routes[:, i : i + 1] == expert).astype(f32) for i in range(2)]
    chosen = [jnp.sum(hit * logits, -1, keepdims=True) for hit in hits]
    top = jnp.maximum(chosen[0], chosen[1])
    powers = [jnp.exp(c - top) for c in chosen]
    share = powers[0] + powers[1]
    gates = hits[0] * (powers[0] / share) + hits[1] * (powers[1] / share)
    hit = hits[0] + hits[1]
    row_at = lax.broadcasted_iota(jnp.int32, (rows, rows), 0)
    col_at = lax.broadcasted_iota(jnp.int32, (rows, rows), 1)
    earlier = (col_at < row_at).astype(bf16)
    rank = jnp.dot(earlier, hit.astype(bf16), preferred_element_type=f32)
    capacity = packed.shape[1]
    slots = lax.broadcasted_iota(jnp.int32, (rows, EXPERTS * capacity), 1).astype(f32)
    placing = jnp.zeros(slots.shape, f32)
    gate = jnp.zeros(slots.shape, f32)
    for e in range(EXPERTS):
        here = (slots == rank[:, e : e + 1] + e * capacity).astype(f32) * hit[:, e : e + 1]
        placing = placing + here
        gate = gate + here * gates[:, e : e + 1]
    weighting[...] = gate
    placing = placing.astype(bf16)
    for j in range(4):
        span = slice(j * width // 4, (j + 1) * width // 4)
        packed[:, :, span] = (
            lax.dot_general(
                placing, normed[:, span], (((0,), (0,)), ((), ())), preferred_element_type=f32
            )
            .astype(bf16)
            .reshape(EXPERTS, capacity, width // 4)
        )
    send.finish()
    sent = inbox.at[pl.ds(0, devices - 1)]
    arrived(sent, scan_send.at[0])
    sent = outbox.at[pl.ds(0, devices - 1)]
    arrived(sent, scan_send.at[1])


def mixer(acts, gains, w_kv, dt_in, dt_out, dt_bias, decay_rate, w_bc, skip_gain, w_router, routes):
    rows, width = acts.shape
    f32, bf16 = jnp.float32, jnp.bfloat16
    dma = pltpu.SemaphoreType.DMA
    whole = pl.BlockSpec(memory_space=pltpu.VMEM)
    apart = pl.BlockSpec(memory_space=pl.ANY)
    capacity = rows * routes.shape[1] // EXPERTS
    grid = (Y_CHIPS, X_CHIPS, 2, 2)
    devices = 2 * X_CHIPS * Y_CHIPS
    blocks = width // 128
    queries = (KVH, HEADS // KVH * rows, HD)
    gather_sems = [dma((2, 3)), dma((2, 3)), dma((2, 2, 3)), dma((2, 2, 3)), dma((2, 4)), dma((2, 4))]
    return pl.pallas_call(
        mixer_kernel,
        out_shape=(
            jax.ShapeDtypeStruct((EXPERTS, capacity, width), bf16),
            jax.ShapeDtypeStruct((rows, EXPERTS * capacity), f32),
            jax.ShapeDtypeStruct((rows, width), f32),
        ),
        in_specs=[whole, whole, whole, apart, apart, whole, whole, apart, whole, apart, whole],
        out_specs=(whole, whole, whole),
        scratch_shapes=[
            pltpu.VMEM(grid + (16, width), bf16),
            pltpu.VMEM(grid + (4, rows, HD), bf16),
            pltpu.VMEM((rows, width), bf16),
            pltpu.VMEM(queries, bf16),
            pltpu.VMEM(queries, f32),
            pltpu.VMEM(queries, f32),
            pltpu.VMEM(queries, f32),
            pltpu.VMEM((rows, width), f32),
            pltpu.VMEM((rows, width), bf16),
            pltpu.VMEM((rows, blocks, 128), f32),
            pltpu.VMEM((rows, blocks, 128), f32),
            pltpu.VMEM((rows, 128), f32),
            pltpu.SMEM((rows, 128), f32),
            pltpu.VMEM((devices, 2, 8, 128), f32),
            pltpu.VMEM((devices, 2, 8, 128), f32),
            pltpu.VMEM((devices, 8, 128), f32),
            pltpu.VMEM((16, blocks, 128), f32),
            pltpu.VMEM(dt_in.shape, bf16),
            pltpu.VMEM(dt_out.shape, bf16),
            pltpu.VMEM(w_bc.shape, bf16),
            pltpu.VMEM(w_router.shape, bf16),
            dma((4,)),
            dma((2,)),
            dma((2,)),
        ]
        + gather_sems
        + gather_sems,
        compiler_params=pltpu.CompilerParams(
            collective_id=2, has_side_effects=True, vmem_limit_bytes=48 * MIB
        ),
        name="mixer",
    )(acts, gains, w_kv, dt_in, dt_out, dt_bias, decay_rate, w_bc, skip_gain, w_router, routes)


def moe_kernel(
    packed,
    weighting,
    second,
    up_any,
    down_any,
    handed,
    out,
    finished,
    rows,
    parts,
    sibling_parts,
    far_parts,
    side_parts,
    up,
    down,
    hidden,
    weight_sem,
    send_y,
    recv_y,
    send_side,
    recv_side,
    send_far,
    recv_far,
    send_core,
    recv_core,
    back_core_send,
    back_core_recv,
    back_far_send,
    back_far_recv,
    back_side_send,
    back_side_recv,
    back_y_send,
    back_y_recv,
    hand_send,
    hand_recv,
):
    y, x, core = coordinates()
    left = lax.rem(x + X_CHIPS - 1, X_CHIPS)
    right = lax.rem(x + 1, X_CHIPS)
    far = lax.rem(x + 2, X_CHIPS)
    chips = (x, left, right, far)
    on_left, on_right, on_core = place(y, left, core), place(y, right, core), place(y, x, 1 - core)
    send = Sender()

    def row_of(k):
        return lax.rem(y + k, Y_CHIPS)

    load_up = pltpu.make_async_copy(up_any, up, weight_sem.at[0])
    load_down = pltpu.make_async_copy(down_any, down, weight_sem.at[1])
    load_up.start()
    load_down.start()
    segment, segments = lax.axis_index("segment"), lax.axis_size("segment")
    ahead = {"segment": lax.rem(segment + 1, segments)}
    behind = {"segment": lax.rem(segment + segments - 1, segments)}
    peers = [on_left, on_right, on_core] + [place(row_of(k), x, core) for k in (1, 2, 3)]
    peers = peers + [ahead, behind]
    greet(peers)
    greeted(len(peers))

    def block(at, k):
        return rows.at[chips[at], core, row_of(k)]

    def own_block(k):
        send(block(0, k), block(0, k), send_side.at[0, k], recv_side.at[0, k], on_right)
        send(block(0, k), block(0, k), send_side.at[1, k], recv_side.at[1, k], on_left)
        send(block(0, k), block(0, k), send_core.at[0, k], recv_core.at[0, k], on_core)

    def side_block(k):
        arrived(block(1, k), recv_side.at[0, k])
        if k in (0, 1):
            send(block(1, k), block(1, k), send_far.at[k], recv_far.at[k], on_right)
        send(block(1, k), block(1, k), send_core.at[1, k], recv_core.at[1, k], on_core)
        arrived(block(2, k), recv_side.at[1, k])
        if k in (2, 3):
            send(block(2, k), block(2, k), send_far.at[k], recv_far.at[k], on_left)
        send(block(2, k), block(2, k), send_core.at[2, k], recv_core.at[2, k], on_core)

    def far_block(k):
        arrived(block(3, k), recv_far.at[k])
        send(block(3, k), block(3, k), send_core.at[3, k], recv_core.at[3, k], on_core)

    def from_core(at):
        for k in range(Y_CHIPS):
            other = rows.at[chips[at], 1 - core, row_of(k)]
            arrived(other, recv_core.at[at, k])

    def experts(at):
        chip = chips[at]

        def one_core(turn, carry):
            which = lax.rem(1 - core + turn, 2)
            taken = rows[chip, which].reshape(-1, rows.shape[-1])
            lifted = jnp.dot(taken, up[...], preferred_element_type=jnp.float32)
            hidden[...] = jax.nn.silu(lifted).astype(jnp.bfloat16)

            def columns(j, carry):
                span = pl.ds(pl.multiple_of(j * 512, 512), 512)
                lowered = jnp.dot(hidden[...], down[:, span], preferred_element_type=jnp.float32)
                parts[chip, which, :, :, span] = lowered.astype(jnp.bfloat16).reshape(
                    Y_CHIPS, -1, 512
                )
                return carry

            return lax.fori_loop(0, rows.shape[-1] // 512, columns, carry)

        lax.fori_loop(0, 2, one_core, 0)
        send(
            parts.at[chip, 1 - core],
            sibling_parts.at[chip],
            back_core_send.at[at],
            back_core_recv.at[at],
            on_core,
        )

    def added(*refs):
        total = refs[0][...].astype(jnp.float32)
        for ref in refs[1:]:
            total = total + ref[...].astype(jnp.float32)
        return total.astype(jnp.bfloat16)

    def mine(at, k):
        return parts.at[chips[at], core, row_of(k)]

    def theirs(at, k):
        return sibling_parts.at[chips[at], row_of(k)]

    for k in (1, 3, 2):
        send(
            packed.at[row_of(k)],
            rows.at[x, core, y],
            send_y.at[k],
            recv_y.at[4 - k],
            place(row_of(k), x, core),
        )
    rows[x, core, y] = packed[y]
    own_block(0)
    for k in (1, 3, 2):
        arrived(block(0, k), recv_y.at[k])
        own_block(k)
    load_up.wait()
    load_down.wait()
    from_core(0)
    side_block(0)
    experts(0)
    for k in (1, 3, 2):
        side_block(k)
    from_core(1)
    experts(1)
    far_block(0)
    from_core(2)
    experts(2)
    for k in (1, 3, 2):
        far_block(k)

    def core_sum(at):
        arrived(sibling_parts.at[chips[at]], back_core_recv.at[at])

    def to_side(at, k, relayed):
        if relayed:
            slot = far_parts.at[k]
            arrived(slot, back_far_recv.at[k])
            mine(at, k)[...] = added(mine(at, k), theirs(at, k), slot)
        else:
            mine(at, k)[...] = added(mine(at, k), theirs(at, k))
        to = on_left if at == 1 else on_right
        send(
            mine(at, k),
            side_parts.at[at - 1, k],
            back_side_send.at[at - 1, k],
            back_side_recv.at[at - 1, k],
            to,
        )

    core_sum(1)
    core_sum(2)
    for k in (3, 0):
        to_side(1, k, False)
    for k in (2, 1):
        to_side(2, k, False)
    from_core(3)
    experts(3)
    core_sum(3)
    for k in (2, 3, 1, 0):
        mine(3, k)[...] = added(mine(3, k), theirs(3, k))
        to = on_left if k in (2, 1) else on_right
        send(mine(3, k), far_parts.at[k], back_far_send.at[k], back_far_recv.at[k], to)
    core_sum(0)
    for k in (2, 3, 1, 0):
        to_side(1 if k in (2, 1) else 2, k, True)
    for k in (2, 3, 1, 0):
        for at in (1, 2):
            arrived(side_parts.at[at - 1, k], back_side_recv.at[at - 1, k])
        total = added(mine(0, k), theirs(0, k), side_parts.at[0, k], side_parts.at[1, k])
        if k == 0:
            out[y] = total
        else:
            mine(0, k)[...] = total
            send(
                mine(0, k),
                out.at[y],
                back_y_send.at[k],
                back_y_recv.at[4 - k],
                place(row_of(k), x, core),
            )
    for k in (1, 3, 2):
        arrived(out.at[row_of(k)], back_y_recv.at[k])
    gate = weighting[...]
    high = gate.astype(jnp.bfloat16)
    low = (gate - high.astype(jnp.float32)).astype(jnp.bfloat16)
    strip = 512
    for j in range(rows.shape[-1] // strip):
        span = pl.ds(j * strip, strip)
        expert_out = out[:, :, span].reshape(-1, strip)
        mixture_rows = jnp.dot(high, expert_out, preferred_element_type=jnp.float32) + jnp.dot(
            low, expert_out, preferred_element_type=jnp.float32
        )
        finished[:, span] = (second[:, span] + mixture_rows).astype(jnp.bfloat16)
        send(finished.at[:, span], handed.at[:, span], hand_send.at[j], hand_recv.at[j], ahead)
    for j in range(rows.shape[-1] // strip):
        arrived(handed.at[:, pl.ds(j * strip, strip)], hand_recv.at[j])
    send.finish()


def mixture(packed, weighting, second, w_up, w_down):
    experts, capacity, width = packed.shape
    units = w_up.shape[1]
    kind = jnp.bfloat16
    block = (capacity, width)
    dma = pltpu.SemaphoreType.DMA
    return pl.pallas_call(
        moe_kernel,
        out_shape=jax.ShapeDtypeStruct(second.shape, kind),
        in_specs=[
            pl.BlockSpec(memory_space=pltpu.VMEM),
            pl.BlockSpec(memory_space=pltpu.VMEM),
            pl.BlockSpec(memory_space=pltpu.VMEM),
            pl.BlockSpec(memory_space=pl.ANY),
            pl.BlockSpec(memory_space=pl.ANY),
        ],
        out_specs=pl.BlockSpec(memory_space=pltpu.VMEM),
        scratch_shapes=[
            pltpu.VMEM(packed.shape, kind),
            pltpu.VMEM(second.shape, kind),
            pltpu.VMEM((X_CHIPS, 2, Y_CHIPS) + block, kind),
            pltpu.VMEM((X_CHIPS, 2, Y_CHIPS) + block, kind),
            pltpu.VMEM((X_CHIPS, Y_CHIPS) + block, kind),
            pltpu.VMEM((Y_CHIPS,) + block, kind),
            pltpu.VMEM((2, Y_CHIPS) + block, kind),
            pltpu.VMEM(w_up.shape, kind),
            pltpu.VMEM(w_down.shape, kind),
            pltpu.VMEM((Y_CHIPS * capacity, units), kind),
            dma((2,)),
            dma((4,)),
            dma((4,)),
            dma((2, 4)),
            dma((2, 4)),
            dma((4,)),
            dma((4,)),
            dma((4, 4)),
            dma((4, 4)),
            dma((4,)),
            dma((4,)),
            dma((4,)),
            dma((4,)),
            dma((2, 4)),
            dma((2, 4)),
            dma((4,)),
            dma((4,)),
            dma((4,)),
            dma((4,)),
        ],
        compiler_params=pltpu.CompilerParams(
            collective_id=1, has_side_effects=True, vmem_limit_bytes=56 * MIB
        ),
        name="mixture",
    )(packed, weighting, second, w_up, w_down)


def on_device(
    acts,
    norm_gains,
    w_kv,
    dt_in,
    dt_out,
    dt_bias,
    decay_rate,
    w_bc,
    skip_gain,
    w_router,
    routes,
    w_up,
    w_down,
):
    packed, weighting, second = mixer(
        acts[0],
        norm_gains[0],
        w_kv[0].T,
        dt_in[0],
        dt_out[0],
        dt_bias,
        decay_rate,
        w_bc[0],
        skip_gain,
        w_router[0],
        routes[0],
    )
    return mixture(packed, weighting, second, w_up[0], w_down[0])[None]


def solution(mesh):
    in_specs = (
        P("segment", "ctx", None),
        P("segment", None, None),
        P("segment", None, "ctx"),
        P("segment", None, None),
        P("segment", None, None),
        P("segment", None),
        P("segment", None),
        P("segment", None, None),
        P("segment", None),
        P("segment", None, None),
        P("segment", "ctx", None),
        P("segment", None, "ctx"),
        P("segment", "ctx", None),
    )
    out_specs = P("segment", "ctx", None)
    return jax.shard_map(
        on_device, mesh=mesh, in_specs=in_specs, out_specs=out_specs, check_vma=False
    )
```

```python
import functools

import jax
import jax.numpy as jnp
from jax import lax
from jax.experimental import pallas as pl
from jax.experimental.pallas import tpu as pltpu
from jax.sharding import PartitionSpec as P

HEADS = 16
KVH = 4
HD = 128
EXPERTS = 4
X_CHIPS = 4
Y_CHIPS = 4
MIB = 1 << 20
LOG2E = 1.4426950408889634


def place(y, x, core):
    return {"ctx": (y * X_CHIPS + x) * 2 + core}


def coordinates():
    ctx = lax.axis_index("ctx")
    return lax.div(ctx, 2 * X_CHIPS), lax.rem(lax.div(ctx, 2), X_CHIPS), lax.rem(ctx, 2)


def arrived(dst, sem):
    pltpu.make_async_copy(dst, dst, sem).wait()


def rms_norm(values, gain):
    return values * lax.rsqrt(jnp.mean(values * values, -1, keepdims=True) + 1e-06) * gain


class Sender:
    def __init__(self):
        self.started = []

    def __call__(self, src, dst, send_sem, recv_sem, to):
        copy = pltpu.make_async_remote_copy(
            src_ref=src,
            dst_ref=dst,
            send_sem=send_sem,
            recv_sem=recv_sem,
            device_id=to,
            device_id_type=pl.DeviceIdType.MESH,
        )
        copy.start()
        self.started.append(copy)

    def both_ways(self, ref, sends, receives, ahead, behind):
        self(ref, ref, sends(0), receives(0), ahead)
        self(ref, ref, sends(1), receives(1), behind)

    def finish(self):
        for copy in self.started:
            copy.wait_send()


class Gather:
    def __init__(self, buf, sems, send):
        self.buf, self.send = buf, send
        self.s1, self.r1, self.s2, self.r2, self.sc, self.rc = sems
        self.y, self.x, self.core = coordinates()
        self.behind, self.ahead = lax.rem(3 + 2 * self.core, 4), lax.rem(1 + 2 * self.core, 4)

    def near(self, half, step, first):
        along_x = (half == 0) == first
        if along_x:
            return place(self.y, lax.rem(self.x + step, X_CHIPS), self.core)
        return place(lax.rem(self.y + step, Y_CHIPS), self.x, self.core)

    def block(self, half, step, item):
        if half == 0:
            return self.buf.at[lax.rem(self.y + step, Y_CHIPS), lax.rem(self.x + item, X_CHIPS), self.core, 0]
        return self.buf.at[lax.rem(self.y + item, Y_CHIPS), lax.rem(self.x + step, X_CHIPS), self.core, 1]

    def line(self, half, step, other=False):
        core = 1 - self.core if other else self.core
        if half == 0:
            return self.buf.at[lax.rem(self.y + step, Y_CHIPS), :, core, 0]
        return self.buf.at[:, lax.rem(self.x + step, X_CHIPS), core, 1]

    def spread(self, half, item):
        self.send.both_ways(
            self.block(half, 0, item),
            lambda i: self.s2.at[half, item, i],
            lambda i: self.r2.at[half, item, i],
            self.near(half, 1, False),
            self.near(half, 3, False),
        )

    def start(self, half):
        self.send.both_ways(
            self.block(half, 0, 0),
            lambda i: self.s1.at[half, i],
            lambda i: self.r1.at[half, i],
            self.near(half, 1, True),
            self.near(half, 3, True),
        )

    def relay(self, half):
        ref = self.block(half, 0, self.behind)
        arrived(ref, self.r1.at[half, self.core])
        to = self.near(half, self.ahead, True)
        self.send(ref, ref, self.s1.at[half, 2], self.r1.at[half, 2], to)
        self.spread(half, self.behind)

    def turn(self, half):
        arrived(self.block(half, 0, self.ahead), self.r1.at[half, 1 - self.core])
        self.spread(half, self.ahead)

    def turn_far(self, half):
        arrived(self.block(half, 0, 2), self.r1.at[half, 2])
        self.spread(half, 2)
        self.share(half, 0)

    def share(self, half, step):
        ref = self.line(half, step)
        to = place(self.y, self.x, 1 - self.core)
        self.send(ref, ref, self.sc.at[half, step], self.rc.at[half, step], to)

    def relay_line(self, half, item):
        ref = self.block(half, self.behind, item)
        arrived(ref, self.r2.at[half, item, self.core])
        to = self.near(half, self.ahead, False)
        self.send(ref, ref, self.s2.at[half, item, 2], self.r2.at[half, item, 2], to)

    def sides(self, half):
        for item in (0, self.behind, self.ahead, 2):
            arrived(self.block(half, self.ahead, item), self.r2.at[half, item, 1 - self.core])
        self.share(half, 3)
        self.share(half, 1)

    def far(self, half):
        for item in (0, self.behind, self.ahead, 2):
            arrived(self.block(half, 2, item), self.r2.at[half, item, 2])
        self.share(half, 2)

    def shared(self, half, step):
        arrived(self.line(half, step, other=True), self.rc.at[half, step])

    def begin(self):
        for step in (self.start, lambda half: self.spread(half, 0), self.relay, self.turn, self.turn_far):
            for half in range(2):
                step(half)

    def pass_on(self):
        for item in (0, self.behind, self.ahead, 2):
            for half in range(2):
                self.relay_line(half, item)


def layer_kernel(names, *refs):
    here = dict(zip(names, refs))
    mix(here)
    experts(here)


def mix(ref):
    y, x, core = coordinates()
    ctx = lax.axis_index("ctx")
    devices = 2 * X_CHIPS * Y_CHIPS
    loaded = ("acts", "gains", "w_kv", "dt_bias", "decay_rate", "skip_gain", "routes")
    loaded = loaded + ("dt_in", "dt_out", "w_bc", "w_router", "up", "down")
    loads = {}
    for i, name in enumerate(loaded):
        loads[name] = pltpu.make_async_copy(ref[name + "_any"], ref[name], ref["load_sem"].at[i])
        loads[name].start()
    ref["loads"] = loads
    segment, segments = lax.axis_index("segment"), lax.axis_size("segment")
    barrier = pltpu.get_barrier_semaphore()

    def hail(step, carry):
        peer = {"ctx": lax.rem(ctx + step, devices)}
        pl.semaphore_signal(barrier, inc=1, device_id=peer, device_id_type=pl.DeviceIdType.MESH)
        return carry

    lax.fori_loop(1, devices, hail, 0)
    for step in (1, segments - 1):
        peer = {"segment": lax.rem(segment + step, segments)}
        pl.semaphore_signal(barrier, inc=1, device_id=peer, device_id_type=pl.DeviceIdType.MESH)
    send = ref["send"] = Sender()
    acts, gains, weights, kv = ref["acts"], ref["gains"], ref["weights"], ref["kv"]
    normed, queries, first, mixed = ref["normed"], ref["queries"], ref["first"], ref["mixed"]
    keep, drive, tail = ref["keep"], ref["drive"], ref["tail"]
    both, both_vmem = ref["both"], ref["both_vmem"]
    second, packed, weighting = ref["second"], ref["packed"], ref["weighting"]
    rows, width = acts.shape
    lanes = 128
    blocks = width // lanes
    f32, bf16 = jnp.float32, jnp.bfloat16

    loads["w_kv"].wait()
    for half in range(2):
        weights[y, x, core, half] = ref["w_kv"][half * 16 : half * 16 + 16]
    pl.semaphore_wait(barrier, devices + 1)
    w_gather = Gather(weights, [ref["w_" + name] for name in GATHER_SEMS], Sender())
    w_gather.start(0)
    w_gather.start(1)
    w_gather.spread(0, 0)
    w_gather.spread(1, 0)
    for name in ("acts", "gains"):
        loads[name].wait()
    normed[...] = rms_norm(acts[...].astype(f32), gains[0]).astype(bf16)
    for step in (w_gather.relay, w_gather.turn, w_gather.turn_far):
        for half in range(2):
            step(half)
    for head in range(HEADS):
        group, place_in = divmod(head, HEADS // KVH)
        queries[group, place_in * rows : (place_in + 1) * rows] = normed[:, head * HD : (head + 1) * HD]
    w_gather.pass_on()
    for step in (w_gather.sides, w_gather.far):
        for half in range(2):
            step(half)
    for half in range(2):
        for step in (0, 3, 1, 2):
            w_gather.shared(half, step)

    for part in range(4):
        made = lax.dot_general(
            normed[...],
            weights[part].reshape(2 * HD, width),
            (((1,), (1,)), ((), ())),
            preferred_element_type=f32,
        ).astype(bf16)
        for head in range(2):
            kv[y, x, core, part % 2, part // 2 * 2 + head] = made[:, head * HD : (head + 1) * HD]

    kv_gather = Gather(kv, [ref["kv_" + name] for name in GATHER_SEMS], send)
    kv_gather.begin()
    group = HEADS // KVH
    keys_here = 2 * X_CHIPS * rows
    queue = lax.broadcasted_iota(jnp.int32, (group, rows, 1), 1).reshape(group * rows, 1) + ctx * rows
    column = lax.broadcasted_iota(jnp.int32, (1, keys_here), 1)

    largest, total, summed = keep, drive, tail

    def of(g):
        return pl.ds(g * (group * rows // blocks), group * rows // blocks)

    def stacked(values):
        return values.reshape(group * rows // blocks, blocks, lanes)

    def attend(half, step):
        kv_gather.shared(half, step)
        if half == 0:
            line = lax.rem(y + step, Y_CHIPS)
            key_pos = column + line * keys_here
        else:
            line = lax.rem(x + step, X_CHIPS)
            per_chip = 2 * rows
            key_pos = column // per_chip * keys_here + line * per_chip + column % per_chip
        allowed = key_pos <= queue

        def one_head(head, carry):
            g = 2 * half + head
            if half == 0:
                k, v = kv[line, :, :, 0, head], kv[line, :, :, 0, 2 + head]
            else:
                k, v = kv[:, line, :, 1, head], kv[:, line, :, 1, 2 + head]
            k, v = k.reshape(keys_here, HD), v.reshape(keys_here, HD)
            scores = lax.dot_general(
                queries[g], k, (((1,), (1,)), ((), ())), preferred_element_type=f32
            ) * (HD**-0.5 * LOG2E)
            scores = jnp.where(allowed, scores, -1e30)
            top = jnp.max(scores, -1, keepdims=True)
            if step == 0:
                newest = jnp.broadcast_to(top, (group * rows, lanes))
            else:
                newest = jnp.maximum(largest[of(g)].reshape(group * rows, lanes), top)
            wide = jnp.concatenate([newest] * (keys_here // lanes), 1)
            probs = jnp.exp2(scores - wide)
            sums = jnp.sum(probs, -1, keepdims=True)
            mixed_in = jnp.dot(probs.astype(bf16), v, preferred_element_type=f32)
            if step == 0:
                total[of(g)] = stacked(jnp.broadcast_to(sums, (group * rows, lanes)))
                summed[of(g)] = stacked(mixed_in)
            else:
                fade = jnp.exp2(largest[of(g)].reshape(group * rows, lanes) - newest)
                total[of(g)] = stacked(total[of(g)].reshape(group * rows, lanes) * fade + sums)
                summed[of(g)] = stacked(summed[of(g)].reshape(group * rows, lanes) * fade + mixed_in)
            largest[of(g)] = stacked(newest)
            return carry

        lax.fori_loop(0, 2, one_head, 0)

    for half in range(2):
        attend(half, 0)
    kv_gather.pass_on()
    w_gather.send.finish()
    for half in range(2):
        kv_gather.sides(half)
    for half in range(2):
        for step in (3, 1):
            attend(half, step)
    for half in range(2):
        kv_gather.far(half)
    for half in range(2):
        attend(half, 2)

    for g in range(KVH):
        made = (summed[of(g)] / total[of(g)]).reshape(group * rows, lanes)
        for r in range(group):
            span = slice((g * group + r) * HD, (g * group + r + 1) * HD)
            first[:, span] = acts[:, span].astype(f32) + made[r * rows : (r + 1) * rows]

    mixed[...] = rms_norm(first[...], gains[1]).astype(bf16)
    for name in loaded:
        if name not in ("acts", "gains", "w_kv", "up", "down"):
            loads[name].wait()
    transposed = (((1,), (1,)), ((), ()))
    both_vmem[:, 0:32] = lax.dot_general(
        mixed[...], ref["w_bc"][...], transposed, preferred_element_type=f32
    )
    to_scalars = pltpu.make_async_copy(both_vmem, both, ref["load_sem"].at[0])
    to_scalars.start()
    states = 16
    b_rows = lax.dot_general(
        ref["w_bc"][0:states], mixed[...], transposed, preferred_element_type=f32
    )
    low_rank = jnp.dot(mixed[...], ref["dt_in"][...], preferred_element_type=f32).astype(bf16)
    for i in range(blocks):
        span = slice(i * lanes, (i + 1) * lanes)
        raw = jnp.dot(low_rank, ref["dt_out"][:, span], preferred_element_type=f32)
        raw = raw + ref["dt_bias"][:, span]
        step_size = jnp.maximum(raw, 0.0) + jnp.log1p(jnp.exp(-jnp.abs(raw)))
        keep[:, i, :] = jnp.exp(-step_size * ref["decay_rate"][:, span])
        drive[:, i, :] = step_size * mixed[:, span].astype(f32)

    def fade(turn, later):
        t = rows - 1 - turn
        tail[t] = drive[t] * later
        return later * keep[t]

    ref["product"][...] = lax.fori_loop(0, rows, fade, jnp.ones((blocks, lanes), f32))

    def two_parts(value):
        high = value.astype(bf16)
        return high, (value - high.astype(f32)).astype(bf16)

    b_high, b_low = two_parts(b_rows)
    b_wide = jnp.concatenate([b_high, b_high, b_low], 1)
    message, inbox, outbox, incoming = ref["message"], ref["inbox"], ref["outbox"], ref["incoming"]
    for i in range(blocks):
        high, low = two_parts(tail[:, i, :])
        ending = jnp.dot(b_wide, jnp.concatenate([high, low, high], 0), preferred_element_type=f32)
        for part in range(2):
            message[2 * i + part, 0] = ending[part * 8 : part * 8 + 8]
            message[2 * i + part, 1] = jnp.broadcast_to(ref["product"][i : i + 1], (8, lanes))

    def swap(mine, theirs, semaphore):
        own = pltpu.make_async_copy(mine(ctx), theirs(ctx), ref["scan_recv"].at[semaphore])
        own.start()

        def one(step, carry):
            peer = lax.rem(ctx + step, devices)
            pltpu.make_async_remote_copy(
                src_ref=mine(peer),
                dst_ref=theirs(ctx),
                send_sem=ref["scan_send"].at[semaphore],
                recv_sem=ref["scan_recv"].at[semaphore],
                device_id={"ctx": peer},
                device_id_type=pl.DeviceIdType.MESH,
            ).start()
            return carry

        lax.fori_loop(1, devices, one, 0)

    def advance(t, carry):
        state, product = carry
        kept, driven = keep[t], drive[t]
        state = tuple(s * kept + driven * both[t, n] for n, s in enumerate(state))
        terms = [s * both[t, states + n] for n, s in enumerate(state)]
        while len(terms) > 1:
            terms = [a + b for a, b in zip(terms[::2], terms[1::2])]
        product = product * kept
        drive[t] = terms[0]
        keep[t] = product
        return state, product

    def join(turn, entering):
        outbox[turn] = entering
        return inbox[turn, 1] * entering + inbox[turn, 0]

    def slot(j):
        return incoming.at[
            pl.ds(pl.multiple_of(lax.rem(j, 2) * 8, 8), 8),
            pl.ds(pl.multiple_of(lax.div(j, 2) * lanes, lanes), lanes),
        ]

    swap(lambda j: message.at[j], lambda j: inbox.at[j], 0)
    to_scalars.wait()
    zero = jnp.zeros((blocks, lanes), f32)
    held = ((zero,) * states, jnp.ones((blocks, lanes), f32))
    held = lax.fori_loop(0, rows // 2, advance, held)
    arrived(inbox, ref["scan_recv"].at[0])
    lax.fori_loop(0, devices, join, jnp.zeros((8, lanes), f32))
    swap(lambda j: outbox.at[j], slot, 1)
    lax.fori_loop(rows // 2, rows, advance, held)
    arrived(incoming, ref["scan_recv"].at[1])
    c_high, c_low = two_parts(both_vmem[:, states : 2 * states])
    c_wide = jnp.concatenate([c_high, c_high, c_low], 1)
    for i in range(blocks):
        span = slice(i * lanes, (i + 1) * lanes)
        high, low = two_parts(incoming[:, span])
        carried = jnp.dot(c_wide, jnp.concatenate([high, low, high], 0), preferred_element_type=f32)
        second[:, span] = (
            first[:, span]
            + drive[:, i, :]
            + keep[:, i, :] * carried
            + ref["skip_gain"][:, span] * mixed[:, span].astype(f32)
        )

    normed[...] = rms_norm(second[...], gains[2]).astype(bf16)
    logits = lax.dot_general(
        ref["w_router"][...], normed[...], transposed, preferred_element_type=f32
    )
    expert = lax.broadcasted_iota(jnp.int32, (EXPERTS, rows), 0)
    hits = [(ref["routes"][i : i + 1] == expert).astype(f32) for i in range(2)]
    chosen = [jnp.sum(hit * logits, 0, keepdims=True) for hit in hits]
    top = jnp.maximum(chosen[0], chosen[1])
    powers = [jnp.exp(c - top) for c in chosen]
    share = powers[0] + powers[1]
    gates = hits[0] * (powers[0] / share) + hits[1] * (powers[1] / share)
    hit = hits[0] + hits[1]
    row_at = lax.broadcasted_iota(jnp.int32, (rows, rows), 0)
    col_at = lax.broadcasted_iota(jnp.int32, (rows, rows), 1)
    earlier = (row_at < col_at).astype(bf16)
    rank = jnp.dot(hit.astype(bf16), earlier, preferred_element_type=f32)
    capacity = rows * 2 // EXPERTS
    slots = lax.broadcasted_iota(jnp.int32, (capacity, rows), 0).astype(f32)
    placing = []
    for e in range(EXPERTS):
        taken = (slots == rank[e : e + 1]).astype(f32) * hit[e : e + 1]
        weighting[e * capacity : (e + 1) * capacity] = taken * gates[e : e + 1]
        placing.append(taken.astype(bf16))
    placing = jnp.concatenate(placing, 0)
    for j in range(4):
        span = slice(j * width // 4, (j + 1) * width // 4)
        packed[:, :, :, :, span] = (
            jnp.dot(placing, normed[:, span], preferred_element_type=f32)
            .astype(bf16)
            .reshape(EXPERTS, 2, 2, 16, width // 4)
        )


def experts(ref):
    y, x, core = coordinates()
    left = lax.rem(x + X_CHIPS - 1, X_CHIPS)
    right = lax.rem(x + 1, X_CHIPS)
    far = lax.rem(x + 2, X_CHIPS)
    chips = (x, left, right, far)
    on_left, on_right, on_core = place(y, left, core), place(y, right, core), place(y, x, 1 - core)
    segments = lax.axis_size("segment")
    ahead = {"segment": lax.rem(lax.axis_index("segment") + 1, segments)}
    send, rows, parts, sibling_parts = ref["send"], ref["rows"], ref["parts"], ref["weights"]
    far_parts, side_parts, hidden, packed = ref["far_parts"], ref["side_parts"], ref["hidden"], ref["packed"]
    out = ref["out"]
    f32, bf16 = jnp.float32, jnp.bfloat16
    capacity, width = far_parts.shape[1:]
    strip = width // 2
    strips = [pl.ds(j * strip, strip) for j in range(2)]

    def row_of(k):
        return lax.rem(y + k, Y_CHIPS)

    def block(at, k):
        return rows.at[chips[at], core, row_of(k)]

    def own_block(k):
        send(block(0, k), block(0, k), ref["send_side"].at[0, k], ref["recv_side"].at[0, k], on_right)
        send(block(0, k), block(0, k), ref["send_side"].at[1, k], ref["recv_side"].at[1, k], on_left)
        send(block(0, k), block(0, k), ref["send_core"].at[0, k], ref["recv_core"].at[0, k], on_core)

    def side_block(k):
        arrived(block(1, k), ref["recv_side"].at[0, k])
        if k in (0, 1):
            send(block(1, k), block(1, k), ref["send_far"].at[k], ref["recv_far"].at[k], on_right)
        send(block(1, k), block(1, k), ref["send_core"].at[1, k], ref["recv_core"].at[1, k], on_core)
        arrived(block(2, k), ref["recv_side"].at[1, k])
        if k in (2, 3):
            send(block(2, k), block(2, k), ref["send_far"].at[k], ref["recv_far"].at[k], on_left)
        send(block(2, k), block(2, k), ref["send_core"].at[2, k], ref["recv_core"].at[2, k], on_core)

    def far_block(k):
        arrived(block(3, k), ref["recv_far"].at[k])
        send(block(3, k), block(3, k), ref["send_core"].at[3, k], ref["recv_core"].at[3, k], on_core)

    def from_core(at):
        for k in range(Y_CHIPS):
            other = rows.at[chips[at], 1 - core, row_of(k)]
            arrived(other, ref["recv_core"].at[at, k])

    def multiply(at):
        chip = chips[at]
        taken = [rows[chip, which].reshape(-1, width) for which in (1 - core, core)]
        lifted = jnp.dot(jnp.concatenate(taken, 0), ref["up"][...], preferred_element_type=f32)
        hidden[...] = jax.nn.silu(lifted).astype(bf16)
        half = hidden.shape[0] // 2
        for j, span in enumerate(strips):
            lowered = jnp.dot(hidden[...], ref["down"][:, span], preferred_element_type=f32)
            lowered = lowered.astype(bf16).reshape(2, Y_CHIPS, capacity, strip)
            rows[chip, 1 - core, :, :, :, :, span] = lowered[0].reshape(Y_CHIPS, 2, 2, 16, strip)
            parts[chip, :, :, span] = lowered[1]
            send(
                rows.at[chip, 1 - core, :, :, :, :, span],
                sibling_parts.at[chip, :, :, :, :, span],
                ref["back_core_send"].at[at, j],
                ref["back_core_recv"].at[at, j],
                on_core,
            )

    def mine(at, k, j):
        return parts.at[chips[at], row_of(k), :, strips[j]]

    def total(at, k, j, *more):
        theirs = sibling_parts[chips[at], row_of(k), :, :, :, strips[j]].reshape(capacity, strip)
        made = mine(at, k, j)[...].astype(f32) + theirs.astype(f32)
        for slot in more:
            made = made + slot[...].astype(f32)
        return made.astype(bf16)

    for k in (1, 3, 2):
        send(
            packed.at[row_of(k)],
            rows.at[x, core, y],
            ref["send_y"].at[k],
            ref["recv_y"].at[4 - k],
            place(row_of(k), x, core),
        )
    rows[x, core, y] = packed[y]
    own_block(0)
    for k in (1, 3, 2):
        arrived(block(0, k), ref["recv_y"].at[k])
        own_block(k)
    side_block(0)
    ref["loads"]["up"].wait()
    ref["loads"]["down"].wait()
    from_core(0)
    multiply(0)
    for k in (1, 3, 2):
        side_block(k)
    from_core(1)
    multiply(1)
    far_block(0)
    from_core(2)
    multiply(2)

    def core_sum(at, j):
        arrived(sibling_parts.at[chips[at], :, :, :, :, strips[j]], ref["back_core_recv"].at[at, j])

    def to_side(at, k, j, relayed):
        more = ()
        if relayed:
            slot = far_parts.at[k, :, strips[j]]
            arrived(slot, ref["back_far_recv"].at[k, j])
            more = (slot,)
        mine(at, k, j)[...] = total(at, k, j, *more)
        send(
            mine(at, k, j),
            side_parts.at[at - 1, k, :, strips[j]],
            ref["back_side_send"].at[at - 1, k, j],
            ref["back_side_recv"].at[at - 1, k, j],
            on_left if at == 1 else on_right,
        )

    for k in (1, 3, 2):
        far_block(k)
    for j in range(2):
        core_sum(1, j)
        core_sum(2, j)
        for k in (3, 0):
            to_side(1, k, j, False)
        for k in (2, 1):
            to_side(2, k, j, False)
    from_core(3)
    multiply(3)
    for j in range(2):
        core_sum(3, j)
        for k in (2, 3, 1, 0):
            mine(3, k, j)[...] = total(3, k, j)
            send(
                mine(3, k, j),
                far_parts.at[k, :, strips[j]],
                ref["back_far_send"].at[k, j],
                ref["back_far_recv"].at[k, j],
                on_left if k in (2, 1) else on_right,
            )
    for j in range(2):
        core_sum(0, j)
        for k in (2, 3, 1, 0):
            to_side(1 if k in (2, 1) else 2, k, j, True)
    gate = ref["weighting"][...]
    high = gate.astype(bf16)
    low = (gate - high.astype(f32)).astype(bf16)
    over_slots = (((0,), (0,)), ((), ()))
    for j, span in enumerate(strips):
        for k in (2, 3, 1, 0):
            sides = [side_parts.at[at, k, :, span] for at in range(2)]
            for at in range(2):
                arrived(sides[at], ref["back_side_recv"].at[at, k, j])
            made = total(0, k, j, *sides)
            if k == 0:
                out[y, :, span] = made
            else:
                mine(0, k, j)[...] = made
                send(
                    mine(0, k, j),
                    out.at[y, :, span],
                    ref["back_y_send"].at[k, j],
                    ref["back_y_recv"].at[4 - k, j],
                    place(row_of(k), x, core),
                )
        for k in (1, 3, 2):
            arrived(out.at[row_of(k), :, span], ref["back_y_recv"].at[k, j])
        expert_out = out[:, :, span].reshape(-1, strip)
        summed = lax.dot_general(high, expert_out, over_slots, preferred_element_type=f32)
        summed = summed + lax.dot_general(low, expert_out, over_slots, preferred_element_type=f32)
        ref["finished"][:, span] = (ref["second"][:, span] + summed).astype(bf16)
        send(
            ref["finished"].at[:, span],
            ref["handed"].at[:, span],
            ref["hand_send"].at[j],
            ref["hand_recv"].at[j],
            ahead,
        )
    for j, span in enumerate(strips):
        arrived(ref["handed"].at[:, span], ref["hand_recv"].at[j])
    send.finish()
    count = 2 * X_CHIPS * Y_CHIPS - 1
    arrived(ref["inbox"].at[pl.ds(0, count)], ref["scan_send"].at[0])
    arrived(ref["outbox"].at[pl.ds(0, count)], ref["scan_send"].at[1])


GATHER_SEMS = {"s1": (2, 3), "r1": (2, 3), "s2": (2, 4, 3), "r2": (2, 4, 3), "sc": (2, 4), "rc": (2, 4)}


def layer(**given):
    rows, width = given["acts"].shape
    units = given["up"].shape[1]
    f32, bf16 = jnp.float32, jnp.bfloat16
    vmem = pltpu.VMEM
    capacity = rows * 2 // EXPERTS
    devices = 2 * X_CHIPS * Y_CHIPS
    blocks = width // 128
    grid = (Y_CHIPS, X_CHIPS, 2, 2)
    block = (capacity, width)
    scratch = {name: vmem(value.shape, value.dtype) for name, value in given.items()}
    scratch |= {
        "weights": vmem(grid + (16, width), bf16),
        "kv": vmem(grid + (4, rows, HD), bf16),
        "normed": vmem((rows, width), bf16),
        "queries": vmem((KVH, HEADS // KVH * rows, HD), bf16),
        "first": vmem((rows, width), f32),
        "mixed": vmem((rows, width), bf16),
        "keep": vmem((rows, blocks, 128), f32),
        "drive": vmem((rows, blocks, 128), f32),
        "tail": vmem((rows, blocks, 128), f32),
        "product": vmem((blocks, 128), f32),
        "both_vmem": vmem((rows, 128), f32),
        "both": pltpu.SMEM((rows, 128), f32),
        "message": vmem((devices, 2, 8, 128), f32),
        "inbox": vmem((devices, 2, 8, 128), f32),
        "outbox": vmem((devices, 8, 128), f32),
        "incoming": vmem((16, width), f32),
        "second": vmem((rows, width), f32),
        "packed": vmem((EXPERTS, 2, 2, 16, width), bf16),
        "weighting": vmem((EXPERTS * capacity, rows), f32),
        "rows": vmem((X_CHIPS, 2, Y_CHIPS, 2, 2, 16, width), bf16),
        "parts": vmem((X_CHIPS, Y_CHIPS) + block, bf16),
        "far_parts": vmem((Y_CHIPS,) + block, bf16),
        "side_parts": vmem((2, Y_CHIPS) + block, bf16),
        "hidden": vmem((2 * Y_CHIPS * capacity, units), bf16),
        "out": vmem((EXPERTS,) + block, bf16),
        "finished": vmem((rows, width), bf16),
    }
    sems = {
        "load_sem": (len(given),),
        "scan_send": (2,),
        "scan_recv": (2,),
        "send_y": (4,),
        "recv_y": (4,),
        "send_side": (2, 4),
        "recv_side": (2, 4),
        "send_far": (4,),
        "recv_far": (4,),
        "send_core": (4, 4),
        "recv_core": (4, 4),
        "back_core_send": (4, 2),
        "back_core_recv": (4, 2),
        "back_far_send": (4, 2),
        "back_far_recv": (4, 2),
        "back_side_send": (2, 4, 2),
        "back_side_recv": (2, 4, 2),
        "back_y_send": (4, 2),
        "back_y_recv": (4, 2),
        "hand_send": (2,),
        "hand_recv": (2,),
    }
    for gather in ("w_", "kv_"):
        sems |= {gather + name: shape for name, shape in GATHER_SEMS.items()}
    scratch |= {name: pltpu.SemaphoreType.DMA(shape) for name, shape in sems.items()}
    names = [name + "_any" for name in given] + ["handed"] + list(scratch)
    return pl.pallas_call(
        functools.partial(layer_kernel, names),
        out_shape=jax.ShapeDtypeStruct((rows, width), bf16),
        in_specs=[pl.BlockSpec(memory_space=pl.ANY)] * len(given),
        out_specs=pl.BlockSpec(memory_space=pltpu.VMEM),
        scratch_shapes=list(scratch.values()),
        compiler_params=pltpu.CompilerParams(
            collective_id=1, has_side_effects=True, vmem_limit_bytes=60 * MIB
        ),
        name="layer",
    )(*given.values())


def on_device(
    acts,
    norm_gains,
    w_kv,
    dt_in,
    dt_out,
    dt_bias,
    decay_rate,
    w_bc,
    skip_gain,
    w_router,
    routes,
    w_up,
    w_down,
):
    return layer(
        acts=acts[0],
        gains=norm_gains.transpose(1, 0, 2),
        w_kv=w_kv[0].T,
        dt_bias=dt_bias,
        decay_rate=decay_rate,
        skip_gain=skip_gain,
        routes=routes[0].T,
        dt_in=dt_in[0],
        dt_out=dt_out[0],
        w_bc=w_bc[0].T,
        w_router=w_router[0].T,
        up=w_up[0],
        down=w_down[0],
    )[None]


def solution(mesh):
    in_specs = (
        P("segment", "ctx", None),
        P("segment", None, None),
        P("segment", None, "ctx"),
        P("segment", None, None),
        P("segment", None, None),
        P("segment", None),
        P("segment", None),
        P("segment", None, None),
        P("segment", None),
        P("segment", None, None),
        P("segment", "ctx", None),
        P("segment", None, "ctx"),
        P("segment", "ctx", None),
    )
    out_specs = P("segment", "ctx", None)
    return jax.shard_map(
        on_device, mesh=mesh, in_specs=in_specs, out_specs=out_specs, check_vma=False
    )
```

```python
import functools
import types

import jax
import jax.numpy as jnp
from jax import lax
from jax.experimental import pallas as pl
from jax.experimental.pallas import tpu as pltpu
from jax.sharding import PartitionSpec as P

HEADS = 16
KVH = 4
HD = 128
EXPERTS = 4
X_CHIPS = 4
Y_CHIPS = 4
MIB = 1 << 20
LOG2E = 1.4426950408889634


def place(y, x, core):
    return {"ctx": (y * X_CHIPS + x) * 2 + core}


def coordinates():
    ctx = lax.axis_index("ctx")
    return lax.div(ctx, 2 * X_CHIPS), lax.rem(lax.div(ctx, 2), X_CHIPS), lax.rem(ctx, 2)


def arrived(dst, sem):
    pltpu.make_async_copy(dst, dst, sem).wait()


def rms_norm(values, gain):
    return values * lax.rsqrt(jnp.mean(values * values, -1, keepdims=True) + 1e-06) * gain


class Sender:
    def __init__(self):
        self.started = []

    def __call__(self, src, dst, send_sem, recv_sem, to):
        copy = pltpu.make_async_remote_copy(
            src_ref=src,
            dst_ref=dst,
            send_sem=send_sem,
            recv_sem=recv_sem,
            device_id=to,
            device_id_type=pl.DeviceIdType.MESH,
        )
        copy.start()
        self.started.append(copy)

    def both_ways(self, ref, sends, receives, ahead, behind):
        self(ref, ref, sends(0), receives(0), ahead)
        self(ref, ref, sends(1), receives(1), behind)

    def finish(self):
        for copy in self.started:
            copy.wait_send()


class Gather:
    def __init__(self, buf, sems, send):
        self.buf, self.send = buf, send
        self.s1, self.r1, self.s2, self.r2, self.sc, self.rc = sems
        self.y, self.x, self.core = coordinates()
        self.behind, self.ahead = lax.rem(3 + 2 * self.core, 4), lax.rem(1 + 2 * self.core, 4)

    def near(self, half, step, first):
        along_x = (half == 0) == first
        if along_x:
            return place(self.y, lax.rem(self.x + step, X_CHIPS), self.core)
        return place(lax.rem(self.y + step, Y_CHIPS), self.x, self.core)

    def block(self, half, step, item):
        if half == 0:
            return self.buf.at[lax.rem(self.y + step, Y_CHIPS), lax.rem(self.x + item, X_CHIPS), self.core, 0]
        return self.buf.at[lax.rem(self.y + item, Y_CHIPS), lax.rem(self.x + step, X_CHIPS), self.core, 1]

    def line(self, half, step, other=False):
        core = 1 - self.core if other else self.core
        if half == 0:
            return self.buf.at[lax.rem(self.y + step, Y_CHIPS), :, core, 0]
        return self.buf.at[:, lax.rem(self.x + step, X_CHIPS), core, 1]

    def spread(self, half, item):
        self.send.both_ways(
            self.block(half, 0, item),
            lambda i: self.s2.at[half, item, i],
            lambda i: self.r2.at[half, item, i],
            self.near(half, 1, False),
            self.near(half, 3, False),
        )

    def start(self, half):
        self.send.both_ways(
            self.block(half, 0, 0),
            lambda i: self.s1.at[half, i],
            lambda i: self.r1.at[half, i],
            self.near(half, 1, True),
            self.near(half, 3, True),
        )

    def relay(self, half):
        ref = self.block(half, 0, self.behind)
        arrived(ref, self.r1.at[half, self.core])
        to = self.near(half, self.ahead, True)
        self.send(ref, ref, self.s1.at[half, 2], self.r1.at[half, 2], to)
        self.spread(half, self.behind)

    def turn(self, half):
        arrived(self.block(half, 0, self.ahead), self.r1.at[half, 1 - self.core])
        self.spread(half, self.ahead)

    def turn_far(self, half):
        arrived(self.block(half, 0, 2), self.r1.at[half, 2])
        self.spread(half, 2)
        self.share(half, 0)

    def share(self, half, step):
        ref = self.line(half, step)
        to = place(self.y, self.x, 1 - self.core)
        self.send(ref, ref, self.sc.at[half, step], self.rc.at[half, step], to)

    def relay_line(self, half, item):
        ref = self.block(half, self.behind, item)
        arrived(ref, self.r2.at[half, item, self.core])
        to = self.near(half, self.ahead, False)
        self.send(ref, ref, self.s2.at[half, item, 2], self.r2.at[half, item, 2], to)

    def sides(self, half):
        for item in (0, self.behind, self.ahead, 2):
            arrived(self.block(half, self.ahead, item), self.r2.at[half, item, 1 - self.core])
        self.share(half, 3)
        self.share(half, 1)

    def far(self, half):
        for item in (0, self.behind, self.ahead, 2):
            arrived(self.block(half, 2, item), self.r2.at[half, item, 2])
        self.share(half, 2)

    def shared(self, half, step):
        arrived(self.line(half, step, other=True), self.rc.at[half, step])

    def begin(self):
        for step in (self.start, lambda half: self.spread(half, 0), self.relay, self.turn, self.turn_far):
            for half in range(2):
                step(half)

    def pass_on(self):
        for item in (0, self.behind, self.ahead, 2):
            for half in range(2):
                self.relay_line(half, item)


def layer_kernel(names, *refs):
    here = types.SimpleNamespace(**dict(zip(names, refs)))
    here.loaded = [name[:-4] for name in names if name[-4:] == "_any"]
    mix(here)
    experts(here)


def mix(ref):
    y, x, core = coordinates()
    ctx = lax.axis_index("ctx")
    devices = 2 * X_CHIPS * Y_CHIPS
    loaded = ref.loaded
    loads = {}
    for i, name in enumerate(loaded):
        loads[name] = pltpu.make_async_copy(getattr(ref, name + "_any"), getattr(ref, name), ref.load_sem.at[i])
        loads[name].start()
    ref.loads = loads
    segment, segments = lax.axis_index("segment"), lax.axis_size("segment")
    barrier = pltpu.get_barrier_semaphore()

    def hail(step, carry):
        peer = {"ctx": lax.rem(ctx + step, devices)}
        pl.semaphore_signal(barrier, inc=1, device_id=peer, device_id_type=pl.DeviceIdType.MESH)
        return carry

    lax.fori_loop(1, devices, hail, 0)
    for step in (1, segments - 1):
        peer = {"segment": lax.rem(segment + step, segments)}
        pl.semaphore_signal(barrier, inc=1, device_id=peer, device_id_type=pl.DeviceIdType.MESH)
    send = ref.send = Sender()
    acts, gains, weights, kv = ref.acts, ref.gains, ref.weights, ref.kv
    normed, queries, first, mixed = ref.normed, ref.queries, ref.first, ref.mixed
    keep, drive, tail = ref.keep, ref.drive, ref.tail
    both, both_vmem = ref.both, ref.both_vmem
    second, packed, weighting = ref.second, ref.packed, ref.weighting
    rows, width = acts.shape
    lanes = 128
    blocks = width // lanes
    f32, bf16 = jnp.float32, jnp.bfloat16

    loads["w_kv"].wait()
    for half in range(2):
        weights[y, x, core, half] = ref.w_kv[half * 16 : half * 16 + 16]
    pl.semaphore_wait(barrier, devices + 1)
    w_gather = Gather(weights, [getattr(ref, "w_" + name) for name in GATHER_SEMS], Sender())
    w_gather.start(0)
    w_gather.start(1)
    w_gather.spread(0, 0)
    w_gather.spread(1, 0)
    for name in ("acts", "gains"):
        loads[name].wait()
    normed[...] = rms_norm(acts[...].astype(f32), gains[0]).astype(bf16)
    for step in (w_gather.relay, w_gather.turn, w_gather.turn_far):
        for half in range(2):
            step(half)
    for head in range(HEADS):
        group, place_in = divmod(head, HEADS // KVH)
        queries[group, place_in * rows : (place_in + 1) * rows] = normed[:, head * HD : (head + 1) * HD]
    w_gather.pass_on()
    for step in (w_gather.sides, w_gather.far):
        for half in range(2):
            step(half)
    for half in range(2):
        for step in (0, 3, 1, 2):
            w_gather.shared(half, step)

    for part in range(4):
        made = lax.dot_general(
            normed[...],
            weights[part].reshape(2 * HD, width),
            (((1,), (1,)), ((), ())),
            preferred_element_type=f32,
        ).astype(bf16)
        for head in range(2):
            kv[y, x, core, part % 2, part // 2 * 2 + head] = made[:, head * HD : (head + 1) * HD]

    kv_gather = Gather(kv, [getattr(ref, "kv_" + name) for name in GATHER_SEMS], send)
    kv_gather.begin()
    group = HEADS // KVH
    keys_here = 2 * X_CHIPS * rows
    queue = lax.broadcasted_iota(jnp.int32, (group, rows, 1), 1).reshape(group * rows, 1) + ctx * rows
    column = lax.broadcasted_iota(jnp.int32, (1, keys_here), 1)

    largest, total, summed = keep, drive, tail

    def of(g):
        return pl.ds(g * (group * rows // blocks), group * rows // blocks)

    def stacked(values):
        return values.reshape(group * rows // blocks, blocks, lanes)

    def attend_half(half, step):
        if half == 0:
            line = lax.rem(y + step, Y_CHIPS)
            key_pos = column + line * keys_here
        else:
            line = lax.rem(x + step, X_CHIPS)
            per_chip = 2 * rows
            key_pos = column // per_chip * keys_here + line * per_chip + column % per_chip
        allowed = key_pos <= queue
        for head in range(2):
            g = 2 * half + head
            if half == 0:
                k, v = kv[line, :, :, 0, head], kv[line, :, :, 0, 2 + head]
            else:
                k, v = kv[:, line, :, 1, head], kv[:, line, :, 1, 2 + head]
            k, v = k.reshape(keys_here, HD), v.reshape(keys_here, HD)
            scores = lax.dot_general(
                queries[g], k, (((1,), (1,)), ((), ())), preferred_element_type=f32
            ) * (HD**-0.5 * LOG2E)
            scores = jnp.where(allowed, scores, -1e30)
            top = jnp.max(scores, -1, keepdims=True)
            if step == 0:
                newest = jnp.broadcast_to(top, (group * rows, lanes))
            else:
                oldest = largest[of(g)].reshape(group * rows, lanes)
                newest = jnp.maximum(oldest, top)
            wide = jnp.concatenate([newest] * (keys_here // lanes), 1)
            probs = jnp.exp2(scores - wide).astype(bf16)
            with_ones = jnp.concatenate([v, jnp.ones_like(v)], 1)
            made = jnp.dot(probs, with_ones, preferred_element_type=f32)
            weighed, sums = made[:, :HD], made[:, HD:]
            if step > 0:
                fade = jnp.exp2(oldest - newest)
                weighed = weighed + summed[of(g)].reshape(group * rows, lanes) * fade
                sums = sums + total[of(g)].reshape(group * rows, lanes) * fade
            summed[of(g)] = stacked(weighed)
            total[of(g)] = stacked(sums)
            largest[of(g)] = stacked(newest)

    def attend(step):
        for half in range(2):
            kv_gather.shared(half, step)
        for half in range(2):
            attend_half(half, step)

    attend(0)
    kv_gather.pass_on()
    w_gather.send.finish()
    for half in range(2):
        kv_gather.sides(half)
    attend(3)
    attend(1)
    for half in range(2):
        kv_gather.far(half)
    attend(2)

    for g in range(KVH):
        made = (summed[of(g)] / total[of(g)]).reshape(group * rows, lanes)
        for r in range(group):
            span = slice((g * group + r) * HD, (g * group + r + 1) * HD)
            first[:, span] = acts[:, span].astype(f32) + made[r * rows : (r + 1) * rows]

    mixed[...] = rms_norm(first[...], gains[1]).astype(bf16)
    for name in loaded[3:-2]:
        loads[name].wait()
    transposed = (((1,), (1,)), ((), ()))
    both_vmem[:, 0:32] = lax.dot_general(
        mixed[...], ref.w_bc[...], transposed, preferred_element_type=f32
    )
    to_scalars = pltpu.make_async_copy(both_vmem, both, ref.load_sem.at[0])
    to_scalars.start()
    states = 16
    b_rows = lax.dot_general(
        ref.w_bc[0:states], mixed[...], transposed, preferred_element_type=f32
    )
    low_rank = jnp.dot(mixed[...], ref.dt_in[...], preferred_element_type=f32).astype(bf16)
    for i in range(blocks):
        span = slice(i * lanes, (i + 1) * lanes)
        raw = jnp.dot(low_rank, ref.dt_out[:, span], preferred_element_type=f32)
        raw = raw + ref.dt_bias[:, span]
        step_size = jnp.maximum(raw, 0.0) + jnp.log1p(jnp.exp(-jnp.abs(raw)))
        keep[:, i, :] = jnp.exp(-step_size * ref.decay_rate[:, span])
        drive[:, i, :] = step_size * mixed[:, span].astype(f32)

    def fade(turn, later):
        t = rows - 1 - turn
        tail[t] = drive[t] * later
        return later * keep[t]

    ref.product[...] = lax.fori_loop(0, rows, fade, jnp.ones((blocks, lanes), f32), unroll=8)

    def two_parts(value):
        high = value.astype(bf16)
        return high, (value - high.astype(f32)).astype(bf16)

    b_high, b_low = two_parts(b_rows)
    b_wide = jnp.concatenate([b_high, b_high, b_low], 1)
    message, inbox, outbox, incoming = ref.message, ref.inbox, ref.outbox, ref.incoming
    for i in range(blocks):
        high, low = two_parts(tail[:, i, :])
        ending = jnp.dot(b_wide, jnp.concatenate([high, low, high], 0), preferred_element_type=f32)
        for part in range(2):
            message[2 * i + part, 0] = ending[part * 8 : part * 8 + 8]
            message[2 * i + part, 1] = jnp.broadcast_to(ref.product[i : i + 1], (8, lanes))

    def swap(mine, theirs, semaphore):
        own = pltpu.make_async_copy(mine(ctx), theirs(ctx), ref.scan_recv.at[semaphore])
        own.start()

        def one(step, carry):
            peer = lax.rem(ctx + step, devices)
            pltpu.make_async_remote_copy(
                src_ref=mine(peer),
                dst_ref=theirs(ctx),
                send_sem=ref.scan_send.at[semaphore],
                recv_sem=ref.scan_recv.at[semaphore],
                device_id={"ctx": peer},
                device_id_type=pl.DeviceIdType.MESH,
            ).start()
            return carry

        lax.fori_loop(1, devices, one, 0)

    def advance(t, carry):
        state, product = carry
        kept, driven = keep[t], drive[t]
        moved, out = [], 0.0
        for n, old in enumerate(state):
            moved.append(old * kept + driven * both[t, n])
            out = out + moved[n] * both[t, states + n]
        product = product * kept
        drive[t] = out
        keep[t] = product
        return tuple(moved), product

    def join(turn, entering):
        outbox[turn] = entering
        return inbox[turn, 1] * entering + inbox[turn, 0]

    def slot(j):
        return incoming.at[
            pl.ds(pl.multiple_of(lax.rem(j, 2) * 8, 8), 8),
            pl.ds(pl.multiple_of(lax.div(j, 2) * lanes, lanes), lanes),
        ]

    swap(lambda j: message.at[j], lambda j: inbox.at[j], 0)
    to_scalars.wait()
    zero = jnp.zeros((blocks, lanes), f32)
    held = ((zero,) * states, jnp.ones((blocks, lanes), f32))
    held = lax.fori_loop(0, rows // 2, advance, held, unroll=8)
    arrived(inbox, ref.scan_recv.at[0])
    lax.fori_loop(0, devices, join, jnp.zeros((8, lanes), f32))
    swap(lambda j: outbox.at[j], slot, 1)
    lax.fori_loop(rows // 2, rows, advance, held, unroll=8)
    arrived(incoming, ref.scan_recv.at[1])
    c_high, c_low = two_parts(both_vmem[:, states : 2 * states])
    c_wide = jnp.concatenate([c_high, c_high, c_low], 1)
    for i in range(blocks):
        span = slice(i * lanes, (i + 1) * lanes)
        high, low = two_parts(incoming[:, span])
        carried = jnp.dot(c_wide, jnp.concatenate([high, low, high], 0), preferred_element_type=f32)
        second[:, span] = (
            first[:, span]
            + drive[:, i, :]
            + keep[:, i, :] * carried
            + ref.skip_gain[:, span] * mixed[:, span].astype(f32)
        )

    normed[...] = rms_norm(second[...], gains[2]).astype(bf16)
    logits = lax.dot_general(
        ref.w_router[...], normed[...], transposed, preferred_element_type=f32
    )
    expert = lax.broadcasted_iota(jnp.int32, (EXPERTS, rows), 0)
    hits = [(ref.routes[i : i + 1] == expert).astype(f32) for i in range(2)]
    chosen = [jnp.sum(hit * logits, 0, keepdims=True) for hit in hits]
    top = jnp.maximum(chosen[0], chosen[1])
    powers = [jnp.exp(c - top) for c in chosen]
    share = powers[0] + powers[1]
    gates = hits[0] * (powers[0] / share) + hits[1] * (powers[1] / share)
    hit = hits[0] + hits[1]
    row_at = lax.broadcasted_iota(jnp.int32, (rows, rows), 0)
    col_at = lax.broadcasted_iota(jnp.int32, (rows, rows), 1)
    earlier = (row_at < col_at).astype(bf16)
    rank = jnp.dot(hit.astype(bf16), earlier, preferred_element_type=f32)
    capacity = rows * 2 // EXPERTS
    slots = lax.broadcasted_iota(jnp.int32, (capacity, rows), 0).astype(f32)
    placing = []
    for e in range(EXPERTS):
        taken = (slots == rank[e : e + 1]).astype(f32) * hit[e : e + 1]
        weighting[e * capacity : (e + 1) * capacity] = taken * gates[e : e + 1]
        placing.append(taken.astype(bf16))
    placing = jnp.concatenate(placing, 0)
    for j in range(4):
        span = slice(j * width // 4, (j + 1) * width // 4)
        packed[:, :, :, :, span] = (
            jnp.dot(placing, normed[:, span], preferred_element_type=f32)
            .astype(bf16)
            .reshape(EXPERTS, 2, 2, 16, width // 4)
        )


def experts(ref):
    y, x, core = coordinates()
    left = lax.rem(x + X_CHIPS - 1, X_CHIPS)
    right = lax.rem(x + 1, X_CHIPS)
    far = lax.rem(x + 2, X_CHIPS)
    chips = (x, left, right, far)
    on_left, on_right, on_core = place(y, left, core), place(y, right, core), place(y, x, 1 - core)
    segments = lax.axis_size("segment")
    ahead = {"segment": lax.rem(lax.axis_index("segment") + 1, segments)}
    send, rows, parts, sibling_parts = ref.send, ref.rows, ref.parts, ref.weights
    far_parts, side_parts, hidden, packed = ref.far_parts, ref.side_parts, ref.hidden, ref.packed
    out = ref.out
    f32, bf16 = jnp.float32, jnp.bfloat16
    capacity, width = far_parts.shape[1:]
    strip = width // 2
    strips = [pl.ds(j * strip, strip) for j in range(2)]

    def row_of(k):
        return lax.rem(y + k, Y_CHIPS)

    def block(at, k):
        return rows.at[chips[at], core, row_of(k)]

    def own_block(k):
        send(block(0, k), block(0, k), ref.send_side.at[0, k], ref.recv_side.at[0, k], on_right)
        send(block(0, k), block(0, k), ref.send_side.at[1, k], ref.recv_side.at[1, k], on_left)
        send(block(0, k), block(0, k), ref.send_core.at[0, k], ref.recv_core.at[0, k], on_core)

    def side_block(k):
        arrived(block(1, k), ref.recv_side.at[0, k])
        if k in (0, 1):
            send(block(1, k), block(1, k), ref.send_far.at[k], ref.recv_far.at[k], on_right)
        send(block(1, k), block(1, k), ref.send_core.at[1, k], ref.recv_core.at[1, k], on_core)
        arrived(block(2, k), ref.recv_side.at[1, k])
        if k in (2, 3):
            send(block(2, k), block(2, k), ref.send_far.at[k], ref.recv_far.at[k], on_left)
        send(block(2, k), block(2, k), ref.send_core.at[2, k], ref.recv_core.at[2, k], on_core)

    def far_block(k):
        arrived(block(3, k), ref.recv_far.at[k])
        send(block(3, k), block(3, k), ref.send_core.at[3, k], ref.recv_core.at[3, k], on_core)

    def from_core(at, steps):
        for k in steps:
            other = rows.at[chips[at], 1 - core, row_of(k)]
            arrived(other, ref.recv_core.at[at, k])

    def multiply(blocks):
        places = [(at, chips[at], row_of(k), k) for at, k in blocks]
        taken = [rows[chip, 1 - core, row].reshape(-1, width) for _, chip, row, _ in places]
        taken = taken + [rows[chip, core, row].reshape(-1, width) for _, chip, row, _ in places]
        count = len(places)
        used = slice(0, 2 * count * capacity)
        lifted = jnp.dot(jnp.concatenate(taken, 0), ref.up[...], preferred_element_type=f32)
        hidden[used] = jax.nn.silu(lifted).astype(bf16)
        for j, span in enumerate(strips):
            lowered = jnp.dot(hidden[used], ref.down[:, span], preferred_element_type=f32)
            lowered = lowered.astype(bf16).reshape(2 * count, capacity, strip)
            for i, (at, chip, row, k) in enumerate(places):
                rows[chip, 1 - core, row, :, :, :, span] = lowered[i].reshape(2, 2, 16, strip)
                parts[chip, row, :, span] = lowered[count + i]
                send(
                    rows.at[chip, 1 - core, row, :, :, :, span],
                    sibling_parts.at[chip, row, :, :, :, span],
                    ref.back_core_send.at[at, k, j],
                    ref.back_core_recv.at[at, k, j],
                    on_core,
                )

    def mine(at, k, j):
        return parts.at[chips[at], row_of(k), :, strips[j]]

    def total(at, k, j, *more):
        theirs = sibling_parts[chips[at], row_of(k), :, :, :, strips[j]].reshape(capacity, strip)
        made = mine(at, k, j)[...].astype(f32) + theirs.astype(f32)
        for slot in more:
            made = made + slot[...].astype(f32)
        return made.astype(bf16)

    def core_sum(at, k, j):
        ended = sibling_parts.at[chips[at], row_of(k), :, :, :, strips[j]]
        arrived(ended, ref.back_core_recv.at[at, k, j])

    def to_side(at, k, j, relayed):
        more = ()
        if relayed:
            slot = far_parts.at[k, :, strips[j]]
            arrived(slot, ref.back_far_recv.at[k, j])
            more = (slot,)
        else:
            core_sum(at, k, j)
        mine(at, k, j)[...] = total(at, k, j, *more)
        send(
            mine(at, k, j),
            side_parts.at[at - 1, k, :, strips[j]],
            ref.back_side_send.at[at - 1, k, j],
            ref.back_side_recv.at[at - 1, k, j],
            on_left if at == 1 else on_right,
        )

    def to_far(k, j):
        core_sum(3, k, j)
        mine(3, k, j)[...] = total(3, k, j)
        send(
            mine(3, k, j),
            far_parts.at[k, :, strips[j]],
            ref.back_far_send.at[k, j],
            ref.back_far_recv.at[k, j],
            on_left if k in (2, 1) else on_right,
        )

    for k in (2, 1, 3):
        send(
            packed.at[row_of(k)],
            rows.at[x, core, y],
            ref.send_y.at[k],
            ref.recv_y.at[4 - k],
            place(row_of(k), x, core),
        )
    rows[x, core, y] = packed[y]
    own_block(0)
    for k in (2, 1, 3):
        arrived(block(0, k), ref.recv_y.at[k])
        own_block(k)
    side_block(0)
    ref.loads["up"].wait()
    ref.loads["down"].wait()
    early, late = (0, 2), (1, 3)
    from_core(0, early + late)
    multiply([(0, k) for k in early + late])
    side_block(2)
    for at in (1, 2):
        from_core(at, early)
    multiply([(at, k) for at in (1, 2) for k in early])
    for k in late:
        side_block(k)
    for at in (1, 2):
        from_core(at, late)
    multiply([(at, k) for at in (1, 2) for k in late])
    for k in early:
        far_block(k)
    for j in range(2):
        to_side(1, 0, j, False)
        to_side(2, 2, j, False)
    from_core(3, early)
    multiply([(3, k) for k in early])
    for k in late:
        far_block(k)
    for j in range(2):
        to_side(1, 3, j, False)
        to_side(2, 1, j, False)
    for j in range(2):
        for k in early:
            to_far(k, j)
    from_core(3, late)
    multiply([(3, k) for k in late])
    for j in range(2):
        for k in late:
            to_far(k, j)
    order = (2, 0, 1, 3)
    for j in range(2):
        for k in order:
            core_sum(1 if k in (2, 1) else 2, k, j)
            to_side(1 if k in (2, 1) else 2, k, j, True)
    gate = ref.weighting[...]
    high = gate.astype(bf16)
    low = (gate - high.astype(f32)).astype(bf16)
    over_slots = (((0,), (0,)), ((), ()))
    for j, span in enumerate(strips):
        for k in order:
            core_sum(0, k, j)
            sides = [side_parts.at[at, k, :, span] for at in range(2)]
            for at in range(2):
                arrived(sides[at], ref.back_side_recv.at[at, k, j])
            made = total(0, k, j, *sides)
            if k == 0:
                out[y, :, span] = made
            else:
                mine(0, k, j)[...] = made
                send(
                    mine(0, k, j),
                    out.at[y, :, span],
                    ref.back_y_send.at[k, j],
                    ref.back_y_recv.at[4 - k, j],
                    place(row_of(k), x, core),
                )
        for k in (2, 1, 3):
            arrived(out.at[row_of(k), :, span], ref.back_y_recv.at[k, j])
        expert_out = out[:, :, span].reshape(-1, strip)
        summed = lax.dot_general(high, expert_out, over_slots, preferred_element_type=f32)
        summed = summed + lax.dot_general(low, expert_out, over_slots, preferred_element_type=f32)
        ref.finished[:, span] = (ref.second[:, span] + summed).astype(bf16)
        send(
            ref.finished.at[:, span],
            ref.handed.at[:, span],
            ref.hand_send.at[j],
            ref.hand_recv.at[j],
            ahead,
        )
    for j, span in enumerate(strips):
        arrived(ref.handed.at[:, span], ref.hand_recv.at[j])
    send.finish()
    count = 2 * X_CHIPS * Y_CHIPS - 1
    arrived(ref.inbox.at[pl.ds(0, count)], ref.scan_send.at[0])
    arrived(ref.outbox.at[pl.ds(0, count)], ref.scan_send.at[1])


GATHER_SEMS = dict(s1=(2, 3), r1=(2, 3), s2=(2, 4, 3), r2=(2, 4, 3), sc=(2, 4), rc=(2, 4))


def layer(**given):
    rows, width = given["acts"].shape
    units = given["up"].shape[1]
    f32, bf16 = jnp.float32, jnp.bfloat16
    vmem = pltpu.VMEM
    capacity = rows * 2 // EXPERTS
    devices = 2 * X_CHIPS * Y_CHIPS
    blocks = width // 128
    grid = (Y_CHIPS, X_CHIPS, 2, 2)
    block = (capacity, width)
    scratch = {name: vmem(value.shape, value.dtype) for name, value in given.items()}
    scratch |= dict(
        weights=vmem(grid + (16, width), bf16),
        kv=vmem(grid + (4, rows, HD), bf16),
        normed=vmem((rows, width), bf16),
        queries=vmem((KVH, HEADS // KVH * rows, HD), bf16),
        first=vmem((rows, width), f32),
        mixed=vmem((rows, width), bf16),
        keep=vmem((rows, blocks, 128), f32),
        drive=vmem((rows, blocks, 128), f32),
        tail=vmem((rows, blocks, 128), f32),
        product=vmem((blocks, 128), f32),
        both_vmem=vmem((rows, 128), f32),
        both=pltpu.SMEM((rows, 128), f32),
        message=vmem((devices, 2, 8, 128), f32),
        inbox=vmem((devices, 2, 8, 128), f32),
        outbox=vmem((devices, 8, 128), f32),
        incoming=vmem((16, width), f32),
        second=vmem((rows, width), f32),
        packed=vmem((EXPERTS, 2, 2, 16, width), bf16),
        weighting=vmem((EXPERTS * capacity, rows), f32),
        rows=vmem((X_CHIPS, 2, Y_CHIPS, 2, 2, 16, width), bf16),
        parts=vmem((X_CHIPS, Y_CHIPS) + block, bf16),
        far_parts=vmem((Y_CHIPS,) + block, bf16),
        side_parts=vmem((2, Y_CHIPS) + block, bf16),
        hidden=vmem((2 * Y_CHIPS * capacity, units), bf16),
        out=vmem((EXPERTS,) + block, bf16),
        finished=vmem((rows, width), bf16),
    )
    sems = dict(
        load_sem=(len(given),),
        scan_send=(2,),
        scan_recv=(2,),
        send_y=(4,),
        recv_y=(4,),
        send_side=(2, 4),
        recv_side=(2, 4),
        send_far=(4,),
        recv_far=(4,),
        send_core=(4, 4),
        recv_core=(4, 4),
        back_core_send=(4, 4, 2),
        back_core_recv=(4, 4, 2),
        back_far_send=(4, 2),
        back_far_recv=(4, 2),
        back_side_send=(2, 4, 2),
        back_side_recv=(2, 4, 2),
        back_y_send=(4, 2),
        back_y_recv=(4, 2),
        hand_send=(2,),
        hand_recv=(2,),
    )
    for gather in ("w_", "kv_"):
        sems |= {gather + name: shape for name, shape in GATHER_SEMS.items()}
    scratch |= {name: pltpu.SemaphoreType.DMA(shape) for name, shape in sems.items()}
    names = [name + "_any" for name in given] + ["handed"] + list(scratch)
    return pl.pallas_call(
        functools.partial(layer_kernel, names),
        out_shape=jax.ShapeDtypeStruct((rows, width), bf16),
        in_specs=[pl.BlockSpec(memory_space=pl.ANY)] * len(given),
        out_specs=pl.BlockSpec(memory_space=pltpu.VMEM),
        scratch_shapes=list(scratch.values()),
        compiler_params=pltpu.CompilerParams(
            collective_id=1, has_side_effects=True, vmem_limit_bytes=60 * MIB
        ),
        name="layer",
    )(*given.values())


def on_device(
    acts,
    norm_gains,
    w_kv,
    dt_in,
    dt_out,
    dt_bias,
    decay_rate,
    w_bc,
    skip_gain,
    w_router,
    routes,
    w_up,
    w_down,
):
    return layer(
        acts=acts[0],
        gains=norm_gains.transpose(1, 0, 2),
        w_kv=w_kv[0].T,
        dt_bias=dt_bias,
        decay_rate=decay_rate,
        skip_gain=skip_gain,
        routes=routes[0].T,
        dt_in=dt_in[0],
        dt_out=dt_out[0],
        w_bc=w_bc[0].T,
        w_router=w_router[0].T,
        up=w_up[0],
        down=w_down[0],
    )[None]


def solution(mesh):
    in_specs = (
        P("segment", "ctx", None),
        P("segment", None, None),
        P("segment", None, "ctx"),
        P("segment", None, None),
        P("segment", None, None),
        P("segment", None),
        P("segment", None),
        P("segment", None, None),
        P("segment", None),
        P("segment", None, None),
        P("segment", "ctx", None),
        P("segment", None, "ctx"),
        P("segment", "ctx", None),
    )
    out_specs = P("segment", "ctx", None)
    return jax.shard_map(
        on_device, mesh=mesh, in_specs=in_specs, out_specs=out_specs, check_vma=False
    )
```

```python
import functools
import types

import jax
import jax.numpy as jnp
from jax import lax
from jax.experimental import pallas as pl
from jax.experimental.pallas import tpu as pltpu
from jax.sharding import PartitionSpec as P

HEADS = 16
KVH = 4
HD = 128
EXPERTS = 4
X_CHIPS = 4
Y_CHIPS = 4
MIB = 1 << 20
LOG2E = 1.4426950408889634


def place(y, x, core):
    return {"ctx": (y * X_CHIPS + x) * 2 + core}


def coordinates():
    ctx = lax.axis_index("ctx")
    return lax.div(ctx, 2 * X_CHIPS), lax.rem(lax.div(ctx, 2), X_CHIPS), lax.rem(ctx, 2)


def arrived(dst, sem):
    pltpu.make_async_copy(dst, dst, sem).wait()


def rms_norm(values, gain):
    return values * lax.rsqrt(jnp.mean(values * values, -1, keepdims=True) + 1e-06) * gain


class Sender:
    def __init__(self):
        self.started = []

    def __call__(self, src, dst, send_sem, recv_sem, to):
        copy = pltpu.make_async_remote_copy(
            src_ref=src,
            dst_ref=dst,
            send_sem=send_sem,
            recv_sem=recv_sem,
            device_id=to,
            device_id_type=pl.DeviceIdType.MESH,
        )
        copy.start()
        self.started.append(copy)

    def both_ways(self, ref, sends, receives, ahead, behind):
        self(ref, ref, sends(0), receives(0), ahead)
        self(ref, ref, sends(1), receives(1), behind)

    def finish(self):
        for copy in self.started:
            copy.wait_send()


class Gather:
    def __init__(self, buf, sems, send):
        self.buf, self.send = buf, send
        self.s1, self.r1, self.s2, self.r2, self.sc, self.rc = sems
        self.y, self.x, self.core = coordinates()
        self.behind, self.ahead = lax.rem(3 + 2 * self.core, 4), lax.rem(1 + 2 * self.core, 4)

    def near(self, half, step, first):
        along_x = (half == 0) == first
        if along_x:
            return place(self.y, lax.rem(self.x + step, X_CHIPS), self.core)
        return place(lax.rem(self.y + step, Y_CHIPS), self.x, self.core)

    def block(self, half, step, item):
        if half == 0:
            return self.buf.at[lax.rem(self.y + step, Y_CHIPS), lax.rem(self.x + item, X_CHIPS), self.core, 0]
        return self.buf.at[lax.rem(self.y + item, Y_CHIPS), lax.rem(self.x + step, X_CHIPS), self.core, 1]

    def line(self, half, step, other=False):
        core = 1 - self.core if other else self.core
        if half == 0:
            return self.buf.at[lax.rem(self.y + step, Y_CHIPS), :, core, 0]
        return self.buf.at[:, lax.rem(self.x + step, X_CHIPS), core, 1]

    def spread(self, half, item):
        self.send.both_ways(
            self.block(half, 0, item),
            lambda i: self.s2.at[half, item, i],
            lambda i: self.r2.at[half, item, i],
            self.near(half, 1, False),
            self.near(half, 3, False),
        )

    def start(self, half):
        self.send.both_ways(
            self.block(half, 0, 0),
            lambda i: self.s1.at[half, i],
            lambda i: self.r1.at[half, i],
            self.near(half, 1, True),
            self.near(half, 3, True),
        )

    def relay(self, half):
        ref = self.block(half, 0, self.behind)
        arrived(ref, self.r1.at[half, self.core])
        to = self.near(half, self.ahead, True)
        self.send(ref, ref, self.s1.at[half, 2], self.r1.at[half, 2], to)
        self.spread(half, self.behind)

    def turn(self, half):
        arrived(self.block(half, 0, self.ahead), self.r1.at[half, 1 - self.core])
        self.spread(half, self.ahead)

    def turn_far(self, half):
        arrived(self.block(half, 0, 2), self.r1.at[half, 2])
        self.spread(half, 2)
        self.share(half, 0)

    def share(self, half, step):
        ref = self.line(half, step)
        to = place(self.y, self.x, 1 - self.core)
        self.send(ref, ref, self.sc.at[half, step], self.rc.at[half, step], to)

    def relay_line(self, half, item):
        ref = self.block(half, self.behind, item)
        arrived(ref, self.r2.at[half, item, self.core])
        to = self.near(half, self.ahead, False)
        self.send(ref, ref, self.s2.at[half, item, 2], self.r2.at[half, item, 2], to)

    def sides(self, half):
        for item in (0, self.behind, self.ahead, 2):
            arrived(self.block(half, self.ahead, item), self.r2.at[half, item, 1 - self.core])
        self.share(half, 3)
        self.share(half, 1)

    def far(self, half):
        for item in (0, self.behind, self.ahead, 2):
            arrived(self.block(half, 2, item), self.r2.at[half, item, 2])
        self.share(half, 2)

    def shared(self, half, step):
        arrived(self.line(half, step, other=True), self.rc.at[half, step])

    def begin(self):
        for step in (self.start, lambda half: self.spread(half, 0), self.relay, self.turn, self.turn_far):
            for half in range(2):
                step(half)

    def pass_on(self):
        for item in (0, self.behind, self.ahead, 2):
            for half in range(2):
                self.relay_line(half, item)


def layer_kernel(names, *refs):
    here = types.SimpleNamespace(**dict(zip(names, refs)))
    here.loaded = [name[:-4] for name in names if name[-4:] == "_any"]
    mix(here)
    experts(here)


def mix(ref):
    y, x, core = coordinates()
    ctx = lax.axis_index("ctx")
    devices = 2 * X_CHIPS * Y_CHIPS
    loaded = ref.loaded
    loads = {}
    for i, name in enumerate(loaded):
        loads[name] = pltpu.make_async_copy(getattr(ref, name + "_any"), getattr(ref, name), ref.load_sem.at[i])
        loads[name].start()
    ref.loads = loads
    segment, segments = lax.axis_index("segment"), lax.axis_size("segment")
    barrier = pltpu.get_barrier_semaphore()

    def hail(step, carry):
        peer = {"ctx": lax.rem(ctx + step, devices)}
        pl.semaphore_signal(barrier, inc=1, device_id=peer, device_id_type=pl.DeviceIdType.MESH)
        return carry

    lax.fori_loop(1, devices, hail, 0)
    for step in (1, segments - 1):
        peer = {"segment": lax.rem(segment + step, segments)}
        pl.semaphore_signal(barrier, inc=1, device_id=peer, device_id_type=pl.DeviceIdType.MESH)
    ref.kv_send = Sender()
    acts, gains, weights, kv = ref.acts, ref.gains, ref.weights, ref.kv
    normed, queries, first, mixed = ref.normed, ref.queries, ref.first, ref.mixed
    keep, drive, tail = ref.keep, ref.drive, ref.tail
    both, both_vmem = ref.both, ref.both_vmem
    second, packed, weighting = ref.second, ref.packed, ref.weighting
    rows, width = acts.shape
    lanes = 128
    blocks = width // lanes
    f32, bf16 = jnp.float32, jnp.bfloat16

    loads["w_kv"].wait()
    for half in range(2):
        weights[y, x, core, half] = ref.w_kv[half * 16 : half * 16 + 16]
    pl.semaphore_wait(barrier, devices + 1)
    w_gather = Gather(weights, [getattr(ref, "w_" + name) for name in GATHER_SEMS], Sender())
    w_gather.start(0)
    w_gather.start(1)
    w_gather.spread(0, 0)
    w_gather.spread(1, 0)
    for name in ("acts", "gains"):
        loads[name].wait()
    normed[...] = rms_norm(acts[...].astype(f32), gains[0]).astype(bf16)
    for step in (w_gather.relay, w_gather.turn, w_gather.turn_far):
        for half in range(2):
            step(half)
    for head in range(HEADS):
        group, place_in = divmod(head, HEADS // KVH)
        queries[group, place_in * rows : (place_in + 1) * rows] = normed[:, head * HD : (head + 1) * HD]
    w_gather.pass_on()
    for step in (w_gather.sides, w_gather.far):
        for half in range(2):
            step(half)
    for half in range(2):
        for step in (0, 3, 1, 2):
            w_gather.shared(half, step)

    for part in range(4):
        made = lax.dot_general(
            normed[...],
            weights[part].reshape(2 * HD, width),
            (((1,), (1,)), ((), ())),
            preferred_element_type=f32,
        ).astype(bf16)
        for head in range(2):
            kv[y, x, core, part % 2, part // 2 * 2 + head] = made[:, head * HD : (head + 1) * HD]

    kv_gather = Gather(kv, [getattr(ref, "kv_" + name) for name in GATHER_SEMS], ref.kv_send)
    kv_gather.begin()
    group = HEADS // KVH
    keys_here = 2 * X_CHIPS * rows
    queue = lax.broadcasted_iota(jnp.int32, (group, rows, 1), 1).reshape(group * rows, 1) + ctx * rows
    column = lax.broadcasted_iota(jnp.int32, (1, keys_here), 1)

    largest, total, summed = keep, drive, tail

    def of(g):
        return pl.ds(g * (group * rows // blocks), group * rows // blocks)

    def stacked(values):
        return values.reshape(group * rows // blocks, blocks, lanes)

    def attend_half(half, step):
        if half == 0:
            line = lax.rem(y + step, Y_CHIPS)
            key_pos = column + line * keys_here
        else:
            line = lax.rem(x + step, X_CHIPS)
            per_chip = 2 * rows
            key_pos = column // per_chip * keys_here + line * per_chip + column % per_chip
        allowed = key_pos <= queue
        for head in range(2):
            g = 2 * half + head
            if half == 0:
                k, v = kv[line, :, :, 0, head], kv[line, :, :, 0, 2 + head]
            else:
                k, v = kv[:, line, :, 1, head], kv[:, line, :, 1, 2 + head]
            k, v = k.reshape(keys_here, HD), v.reshape(keys_here, HD)
            scores = lax.dot_general(
                queries[g], k, (((1,), (1,)), ((), ())), preferred_element_type=f32
            ) * (HD**-0.5 * LOG2E)
            scores = jnp.where(allowed, scores, -1e30)
            top = jnp.max(scores, -1, keepdims=True)
            if step == 0:
                newest = jnp.broadcast_to(top, (group * rows, lanes))
            else:
                oldest = largest[of(g)].reshape(group * rows, lanes)
                newest = jnp.maximum(oldest, top)
            wide = jnp.concatenate([newest] * (keys_here // lanes), 1)
            probs = jnp.exp2(scores - wide).astype(bf16)
            with_ones = jnp.concatenate([v, jnp.ones_like(v)], 1)
            made = jnp.dot(probs, with_ones, preferred_element_type=f32)
            weighed, sums = made[:, :HD], made[:, HD:]
            if step > 0:
                fade = jnp.exp2(oldest - newest)
                weighed = weighed + summed[of(g)].reshape(group * rows, lanes) * fade
                sums = sums + total[of(g)].reshape(group * rows, lanes) * fade
            summed[of(g)] = stacked(weighed)
            total[of(g)] = stacked(sums)
            largest[of(g)] = stacked(newest)

    def attend(step):
        for half in range(2):
            kv_gather.shared(half, step)
        for half in range(2):
            attend_half(half, step)

    attend(0)
    kv_gather.pass_on()
    w_gather.send.finish()
    for half in range(2):
        kv_gather.sides(half)
    attend(3)
    for half in range(2):
        kv_gather.far(half)
    attend(1)
    attend(2)

    for g in range(KVH):
        made = (summed[of(g)] / total[of(g)]).reshape(group * rows, lanes)
        for r in range(group):
            span = slice((g * group + r) * HD, (g * group + r + 1) * HD)
            first[:, span] = acts[:, span].astype(f32) + made[r * rows : (r + 1) * rows]

    mixed[...] = rms_norm(first[...], gains[1]).astype(bf16)
    for name in loaded[3:-2]:
        loads[name].wait()
    transposed = (((1,), (1,)), ((), ()))
    both_vmem[:, 0:32] = lax.dot_general(
        mixed[...], ref.w_bc[...], transposed, preferred_element_type=f32
    )
    to_scalars = pltpu.make_async_copy(both_vmem, both, ref.load_sem.at[0])
    to_scalars.start()
    states = 16
    b_rows = lax.dot_general(
        ref.w_bc[0:states], mixed[...], transposed, preferred_element_type=f32
    )
    low_rank = jnp.dot(mixed[...], ref.dt_in[...], preferred_element_type=f32).astype(bf16)
    for i in range(blocks):
        span = slice(i * lanes, (i + 1) * lanes)
        raw = jnp.dot(low_rank, ref.dt_out[:, span], preferred_element_type=f32)
        raw = raw + ref.dt_bias[:, span]
        step_size = jnp.maximum(raw, 0.0) + jnp.log1p(jnp.exp(-jnp.abs(raw)))
        keep[:, i, :] = jnp.exp(-step_size * ref.decay_rate[:, span])
        drive[:, i, :] = step_size * mixed[:, span].astype(f32)

    def fade(turn, later):
        t = rows - 1 - turn
        tail[t] = drive[t] * later
        return later * keep[t]

    ref.product[...] = lax.fori_loop(0, rows, fade, jnp.ones((blocks, lanes), f32), unroll=8)

    def two_parts(value):
        high = value.astype(bf16)
        return high, (value - high.astype(f32)).astype(bf16)

    b_high, b_low = two_parts(b_rows)
    b_wide = jnp.concatenate([b_high, b_high, b_low], 1)
    message, inbox, outbox, incoming = ref.message, ref.inbox, ref.outbox, ref.incoming
    for i in range(blocks):
        high, low = two_parts(tail[:, i, :])
        ending = jnp.dot(b_wide, jnp.concatenate([high, low, high], 0), preferred_element_type=f32)
        for part in range(2):
            message[2 * i + part, 0] = ending[part * 8 : part * 8 + 8]
            message[2 * i + part, 1] = jnp.broadcast_to(ref.product[i : i + 1], (8, lanes))

    def swap(mine, theirs, semaphore):
        own = pltpu.make_async_copy(mine(ctx), theirs(ctx), ref.scan_recv.at[semaphore])
        own.start()

        def one(step, carry):
            peer = lax.rem(ctx + step, devices)
            pltpu.make_async_remote_copy(
                src_ref=mine(peer),
                dst_ref=theirs(ctx),
                send_sem=ref.scan_send.at[semaphore],
                recv_sem=ref.scan_recv.at[semaphore],
                device_id={"ctx": peer},
                device_id_type=pl.DeviceIdType.MESH,
            ).start()
            return carry

        lax.fori_loop(1, devices, one, 0)

    def advance(t, carry):
        state, product = carry
        kept, driven = keep[t], drive[t]
        moved, out = [], 0.0
        for n, old in enumerate(state):
            moved.append(old * kept + driven * both[t, n])
            out = out + moved[n] * both[t, states + n]
        product = product * kept
        drive[t] = out
        keep[t] = product
        return tuple(moved), product

    def join(turn, entering):
        outbox[turn] = entering
        return inbox[turn, 1] * entering + inbox[turn, 0]

    def slot(j):
        return incoming.at[
            pl.ds(pl.multiple_of(lax.rem(j, 2) * 8, 8), 8),
            pl.ds(pl.multiple_of(lax.div(j, 2) * lanes, lanes), lanes),
        ]

    swap(lambda j: message.at[j], lambda j: inbox.at[j], 0)
    to_scalars.wait()
    zero = jnp.zeros((blocks, lanes), f32)
    held = ((zero,) * states, jnp.ones((blocks, lanes), f32))
    held = lax.fori_loop(0, rows // 2, advance, held, unroll=8)
    arrived(inbox, ref.scan_recv.at[0])
    lax.fori_loop(0, devices, join, jnp.zeros((8, lanes), f32))
    swap(lambda j: outbox.at[j], slot, 1)
    lax.fori_loop(rows // 2, rows, advance, held, unroll=8)
    arrived(incoming, ref.scan_recv.at[1])
    c_high, c_low = two_parts(both_vmem[:, states : 2 * states])
    c_wide = jnp.concatenate([c_high, c_high, c_low], 1)
    for i in range(blocks):
        span = slice(i * lanes, (i + 1) * lanes)
        high, low = two_parts(incoming[:, span])
        carried = jnp.dot(c_wide, jnp.concatenate([high, low, high], 0), preferred_element_type=f32)
        second[:, span] = (
            first[:, span]
            + drive[:, i, :]
            + keep[:, i, :] * carried
            + ref.skip_gain[:, span] * mixed[:, span].astype(f32)
        )

    normed[...] = rms_norm(second[...], gains[2]).astype(bf16)
    logits = lax.dot_general(
        ref.w_router[...], normed[...], transposed, preferred_element_type=f32
    )
    expert = lax.broadcasted_iota(jnp.int32, (EXPERTS, rows), 0)
    hits = [(ref.routes[i : i + 1] == expert).astype(f32) for i in range(2)]
    chosen = [jnp.sum(hit * logits, 0, keepdims=True) for hit in hits]
    top = jnp.maximum(chosen[0], chosen[1])
    powers = [jnp.exp(c - top) for c in chosen]
    share = powers[0] + powers[1]
    gates = hits[0] * (powers[0] / share) + hits[1] * (powers[1] / share)
    hit = hits[0] + hits[1]
    row_at = lax.broadcasted_iota(jnp.int32, (rows, rows), 0)
    col_at = lax.broadcasted_iota(jnp.int32, (rows, rows), 1)
    earlier = (row_at < col_at).astype(bf16)
    rank = jnp.dot(hit.astype(bf16), earlier, preferred_element_type=f32)
    capacity = rows * 2 // EXPERTS
    slots = lax.broadcasted_iota(jnp.int32, (capacity, rows), 0).astype(f32)
    placing = []
    for e in range(EXPERTS):
        taken = (slots == rank[e : e + 1]).astype(f32) * hit[e : e + 1]
        weighting[e * capacity : (e + 1) * capacity] = taken * gates[e : e + 1]
        placing.append(taken.astype(bf16))
    placing = jnp.concatenate(placing, 0)
    for j in range(4):
        span = slice(j * width // 4, (j + 1) * width // 4)
        packed[:, :, :, :, span] = (
            jnp.dot(placing, normed[:, span], preferred_element_type=f32)
            .astype(bf16)
            .reshape(EXPERTS, 2, 2, 16, width // 4)
        )


def experts(ref):
    y, x, core = coordinates()
    left = lax.rem(x + X_CHIPS - 1, X_CHIPS)
    right = lax.rem(x + 1, X_CHIPS)
    far = lax.rem(x + 2, X_CHIPS)
    chips = (x, left, right, far)
    on_left, on_right, on_core = place(y, left, core), place(y, right, core), place(y, x, 1 - core)
    segments = lax.axis_size("segment")
    ahead = {"segment": lax.rem(lax.axis_index("segment") + 1, segments)}
    send, send_back, send_last = Sender(), Sender(), Sender()
    rows, parts, sibling_parts = ref.rows, ref.parts, ref.weights
    far_parts, side_parts, hidden, packed = ref.far_parts, ref.side_parts, ref.hidden, ref.packed
    out = ref.out
    f32, bf16 = jnp.float32, jnp.bfloat16
    capacity, width = far_parts.shape[1:]
    strip = width // 2
    strips = [pl.ds(j * strip, strip) for j in range(2)]

    def row_of(k):
        return lax.rem(y + k, Y_CHIPS)

    def block(at, k):
        return rows.at[chips[at], core, row_of(k)]

    def own_block(k):
        send(block(0, k), block(0, k), ref.send_side.at[0, k], ref.recv_side.at[0, k], on_right)
        send(block(0, k), block(0, k), ref.send_side.at[1, k], ref.recv_side.at[1, k], on_left)
        send(block(0, k), block(0, k), ref.send_core.at[0, k], ref.recv_core.at[0, k], on_core)

    def side_block(k):
        arrived(block(1, k), ref.recv_side.at[0, k])
        if k in (0, 1):
            send(block(1, k), block(1, k), ref.send_far.at[k], ref.recv_far.at[k], on_right)
        send(block(1, k), block(1, k), ref.send_core.at[1, k], ref.recv_core.at[1, k], on_core)
        arrived(block(2, k), ref.recv_side.at[1, k])
        if k in (2, 3):
            send(block(2, k), block(2, k), ref.send_far.at[k], ref.recv_far.at[k], on_left)
        send(block(2, k), block(2, k), ref.send_core.at[2, k], ref.recv_core.at[2, k], on_core)

    def far_block(k):
        arrived(block(3, k), ref.recv_far.at[k])
        send(block(3, k), block(3, k), ref.send_core.at[3, k], ref.recv_core.at[3, k], on_core)

    def from_core(at, steps):
        for k in steps:
            other = rows.at[chips[at], 1 - core, row_of(k)]
            arrived(other, ref.recv_core.at[at, k])

    def multiply(blocks):
        places = [(at, chips[at], row_of(k), k) for at, k in blocks]
        taken = [rows[chip, 1 - core, row].reshape(-1, width) for _, chip, row, _ in places]
        taken = taken + [rows[chip, core, row].reshape(-1, width) for _, chip, row, _ in places]
        count = len(places)
        used = slice(0, 2 * count * capacity)
        lifted = jnp.dot(jnp.concatenate(taken, 0), ref.up[...], preferred_element_type=f32)
        hidden[used] = jax.nn.silu(lifted).astype(bf16)
        for j, span in enumerate(strips):
            lowered = jnp.dot(hidden[used], ref.down[:, span], preferred_element_type=f32)
            lowered = lowered.astype(bf16).reshape(2 * count, capacity, strip)
            for i, (at, chip, row, k) in enumerate(places):
                rows[chip, 1 - core, row, :, :, :, span] = lowered[i].reshape(2, 2, 16, strip)
                parts[chip, row, :, span] = lowered[count + i]
                send_back(
                    rows.at[chip, 1 - core, row, :, :, :, span],
                    sibling_parts.at[chip, row, :, :, :, span],
                    ref.back_core_send.at[at, k, j],
                    ref.back_core_recv.at[at, k, j],
                    on_core,
                )

    thirds = [pl.ds(0, strip), pl.ds(strip, strip // 2), pl.ds(strip + strip // 2, strip // 2)]

    def mine(at, k, span):
        return parts.at[chips[at], row_of(k), :, span]

    def total(at, k, span, *more):
        theirs = sibling_parts[chips[at], row_of(k), :, :, :, span].reshape(capacity, span.size)
        made = mine(at, k, span)[...].astype(f32) + theirs.astype(f32)
        for slot in more:
            made = made + slot[...].astype(f32)
        return made.astype(bf16)

    def core_sum(at, k, j):
        ended = sibling_parts.at[chips[at], row_of(k), :, :, :, strips[j]]
        arrived(ended, ref.back_core_recv.at[at, k, j])

    def to_side(at, k, j):
        core_sum(at, k, j)
        mine(at, k, strips[j])[...] = total(at, k, strips[j])
        send_back(
            mine(at, k, strips[j]),
            side_parts.at[at - 1, k, :, strips[j]],
            ref.back_side_send.at[k, j],
            ref.back_side_recv.at[k, j],
            on_left if at == 1 else on_right,
        )

    def to_far(k, j):
        core_sum(3, k, j)
        mine(3, k, strips[j])[...] = total(3, k, strips[j])
        send_back(
            mine(3, k, strips[j]),
            far_parts.at[k, :, strips[j]],
            ref.back_far_send.at[k, j],
            ref.back_far_recv.at[k, j],
            on_left if k in (2, 1) else on_right,
        )

    def pass_on(k, j):
        at, span = 1 if k in (2, 1) else 2, thirds[j]
        if j < 2:
            core_sum(at, k, j)
            arrived(far_parts.at[k, :, strips[j]], ref.back_far_recv.at[k, j])
        mine(at, k, span)[...] = total(at, k, span, far_parts.at[k, :, span])
        send_last(
            mine(at, k, span),
            side_parts.at[at - 1, k, :, span],
            ref.back_relay_send.at[k, j],
            ref.back_relay_recv.at[k, j],
            on_left if at == 1 else on_right,
        )

    for k in (2, 1, 3):
        send(
            packed.at[row_of(k)],
            rows.at[x, core, y],
            ref.send_y.at[k],
            ref.recv_y.at[4 - k],
            place(row_of(k), x, core),
        )
    rows[x, core, y] = packed[y]
    own_block(0)
    for k in (2, 1, 3):
        arrived(block(0, k), ref.recv_y.at[k])
        own_block(k)
    count = 2 * X_CHIPS * Y_CHIPS - 1
    arrived(ref.inbox.at[pl.ds(0, count)], ref.scan_send.at[0])
    arrived(ref.outbox.at[pl.ds(0, count)], ref.scan_send.at[1])
    ref.kv_send.finish()
    side_block(0)
    ref.loads["up"].wait()
    ref.loads["down"].wait()
    early, late = (0, 2), (1, 3)
    from_core(0, early + late)
    multiply([(0, k) for k in early + late])
    side_block(2)
    for at in (1, 2):
        from_core(at, early)
    multiply([(at, k) for at in (1, 2) for k in early])
    for k in late:
        side_block(k)
    for at in (1, 2):
        from_core(at, late)
    multiply([(at, k) for at in (1, 2) for k in late])
    for k in early:
        far_block(k)
    for j in range(2):
        to_side(1, 0, j)
        to_side(2, 2, j)
    from_core(3, early)
    multiply([(3, k) for k in early])
    for k in late:
        far_block(k)
    for j in range(2):
        to_side(1, 3, j)
        to_side(2, 1, j)
    for j in range(2):
        for k in early:
            to_far(k, j)
    from_core(3, late)
    multiply([(3, k) for k in late])
    for j in range(2):
        for k in late:
            to_far(k, j)
    send.finish()
    order = (2, 0, 1, 3)
    for j in range(3):
        for k in order:
            pass_on(k, j)
    send_back.finish()
    gate = ref.weighting[...]
    high = gate.astype(bf16)
    low = (gate - high.astype(f32)).astype(bf16)
    over_slots = (((0,), (0,)), ((), ()))
    for j, span in enumerate(thirds):
        for k in order:
            relayed = 0 if k in (2, 1) else 1
            if j < 2:
                core_sum(0, k, j)
                arrived(side_parts.at[1 - relayed, k, :, strips[j]], ref.back_side_recv.at[k, j])
            arrived(side_parts.at[relayed, k, :, span], ref.back_relay_recv.at[k, j])
            made = total(0, k, span, side_parts.at[0, k, :, span], side_parts.at[1, k, :, span])
            if k == 0:
                out[y, :, span] = made
            else:
                mine(0, k, span)[...] = made
                send_last(
                    mine(0, k, span),
                    out.at[y, :, span],
                    ref.back_y_send.at[k, j],
                    ref.back_y_recv.at[4 - k, j],
                    place(row_of(k), x, core),
                )
        for k in (2, 1, 3):
            arrived(out.at[row_of(k), :, span], ref.back_y_recv.at[k, j])
        expert_out = out[:, :, span].reshape(-1, span.size)
        summed = lax.dot_general(high, expert_out, over_slots, preferred_element_type=f32)
        summed = summed + lax.dot_general(low, expert_out, over_slots, preferred_element_type=f32)
        ref.finished[:, span] = (ref.second[:, span] + summed).astype(bf16)
        send_last(
            ref.finished.at[:, span],
            ref.handed.at[:, span],
            ref.hand_send.at[j],
            ref.hand_recv.at[j],
            ahead,
        )
    for j, span in enumerate(thirds):
        arrived(ref.handed.at[:, span], ref.hand_recv.at[j])
    send_last.finish()


GATHER_SEMS = dict(s1=(2, 3), r1=(2, 3), s2=(2, 4, 3), r2=(2, 4, 3), sc=(2, 4), rc=(2, 4))


def layer(**given):
    rows, width = given["acts"].shape
    units = given["up"].shape[1]
    f32, bf16 = jnp.float32, jnp.bfloat16
    vmem = pltpu.VMEM
    capacity = rows * 2 // EXPERTS
    devices = 2 * X_CHIPS * Y_CHIPS
    blocks = width // 128
    grid = (Y_CHIPS, X_CHIPS, 2, 2)
    block = (capacity, width)
    scratch = {name: vmem(value.shape, value.dtype) for name, value in given.items()}
    scratch |= dict(
        weights=vmem(grid + (16, width), bf16),
        kv=vmem(grid + (4, rows, HD), bf16),
        normed=vmem((rows, width), bf16),
        queries=vmem((KVH, HEADS // KVH * rows, HD), bf16),
        first=vmem((rows, width), f32),
        mixed=vmem((rows, width), bf16),
        keep=vmem((rows, blocks, 128), f32),
        drive=vmem((rows, blocks, 128), f32),
        tail=vmem((rows, blocks, 128), f32),
        product=vmem((blocks, 128), f32),
        both_vmem=vmem((rows, 128), f32),
        both=pltpu.SMEM((rows, 128), f32),
        message=vmem((devices, 2, 8, 128), f32),
        inbox=vmem((devices, 2, 8, 128), f32),
        outbox=vmem((devices, 8, 128), f32),
        incoming=vmem((16, width), f32),
        second=vmem((rows, width), f32),
        packed=vmem((EXPERTS, 2, 2, 16, width), bf16),
        weighting=vmem((EXPERTS * capacity, rows), f32),
        rows=vmem((X_CHIPS, 2, Y_CHIPS, 2, 2, 16, width), bf16),
        parts=vmem((X_CHIPS, Y_CHIPS) + block, bf16),
        far_parts=vmem((Y_CHIPS,) + block, bf16),
        side_parts=vmem((2, Y_CHIPS) + block, bf16),
        hidden=vmem((2 * Y_CHIPS * capacity, units), bf16),
        out=vmem((EXPERTS,) + block, bf16),
        finished=vmem((rows, width), bf16),
    )
    sems = dict(
        load_sem=(len(given),),
        scan_send=(2,),
        scan_recv=(2,),
        send_y=(4,),
        recv_y=(4,),
        send_side=(2, 4),
        recv_side=(2, 4),
        send_far=(4,),
        recv_far=(4,),
        send_core=(4, 4),
        recv_core=(4, 4),
        back_core_send=(4, 4, 2),
        back_core_recv=(4, 4, 2),
        back_far_send=(4, 2),
        back_far_recv=(4, 2),
        back_side_send=(4, 2),
        back_side_recv=(4, 2),
        back_relay_send=(4, 3),
        back_relay_recv=(4, 3),
        back_y_send=(4, 3),
        back_y_recv=(4, 3),
        hand_send=(3,),
        hand_recv=(3,),
    )
    for gather in ("w_", "kv_"):
        sems |= {gather + name: shape for name, shape in GATHER_SEMS.items()}
    scratch |= {name: pltpu.SemaphoreType.DMA(shape) for name, shape in sems.items()}
    names = [name + "_any" for name in given] + ["handed"] + list(scratch)
    return pl.pallas_call(
        functools.partial(layer_kernel, names),
        out_shape=jax.ShapeDtypeStruct((rows, width), bf16),
        in_specs=[pl.BlockSpec(memory_space=pl.ANY)] * len(given),
        out_specs=pl.BlockSpec(memory_space=pltpu.VMEM),
        scratch_shapes=list(scratch.values()),
        compiler_params=pltpu.CompilerParams(
            collective_id=1, has_side_effects=True, vmem_limit_bytes=60 * MIB
        ),
        name="layer",
    )(*given.values())


def on_device(
    acts,
    norm_gains,
    w_kv,
    dt_in,
    dt_out,
    dt_bias,
    decay_rate,
    w_bc,
    skip_gain,
    w_router,
    routes,
    w_up,
    w_down,
):
    return layer(
        acts=acts[0],
        gains=norm_gains.transpose(1, 0, 2),
        w_kv=w_kv[0].T,
        dt_bias=dt_bias,
        decay_rate=decay_rate,
        skip_gain=skip_gain,
        routes=routes[0].T,
        dt_in=dt_in[0],
        dt_out=dt_out[0],
        w_bc=w_bc[0].T,
        w_router=w_router[0].T,
        up=w_up[0],
        down=w_down[0],
    )[None]


def solution(mesh):
    in_specs = (
        P("segment", "ctx", None),
        P("segment", None, None),
        P("segment", None, "ctx"),
        P("segment", None, None),
        P("segment", None, None),
        P("segment", None),
        P("segment", None),
        P("segment", None, None),
        P("segment", None),
        P("segment", None, None),
        P("segment", "ctx", None),
        P("segment", None, "ctx"),
        P("segment", "ctx", None),
    )
    out_specs = P("segment", "ctx", None)
    return jax.shard_map(
        on_device, mesh=mesh, in_specs=in_specs, out_specs=out_specs, check_vma=False
    )
```

```python
import functools
import types

import jax
import jax.numpy as jnp
from jax import lax
from jax.experimental import pallas as pl
from jax.experimental.pallas import tpu as pltpu
from jax.sharding import PartitionSpec as P

HEADS = 16
KVH = 4
HD = 128
EXPERTS = 4
X_CHIPS = 4
Y_CHIPS = 4
MIB = 1 << 20
LOG2E = 1.4426950408889634


def place(y, x, core):
    return {"ctx": (y * X_CHIPS + x) * 2 + core}


def coordinates():
    ctx = lax.axis_index("ctx")
    return lax.div(ctx, 2 * X_CHIPS), lax.rem(lax.div(ctx, 2), X_CHIPS), lax.rem(ctx, 2)


def arrived(dst, sem):
    pltpu.make_async_copy(dst, dst, sem).wait()


def rms_norm(values, gain):
    return values * lax.rsqrt(jnp.mean(values * values, -1, keepdims=True) + 1e-06) * gain


class Sender:
    def __init__(self):
        self.started = []

    def __call__(self, src, dst, send_sem, recv_sem, to):
        copy = pltpu.make_async_remote_copy(
            src_ref=src,
            dst_ref=dst,
            send_sem=send_sem,
            recv_sem=recv_sem,
            device_id=to,
            device_id_type=pl.DeviceIdType.MESH,
        )
        copy.start()
        self.started.append(copy)

    def both_ways(self, ref, sends, receives, ahead, behind):
        self(ref, ref, sends(0), receives(0), ahead)
        self(ref, ref, sends(1), receives(1), behind)

    def finish(self):
        for copy in self.started:
            copy.wait_send()


class Gather:
    def __init__(self, buf, sems, send):
        self.buf, self.send = buf, send
        self.s1, self.r1, self.s2, self.r2, self.sc, self.rc = sems
        self.y, self.x, self.core = coordinates()
        self.behind, self.ahead = lax.rem(3 + 2 * self.core, 4), lax.rem(1 + 2 * self.core, 4)

    def near(self, half, step, first):
        along_x = (half == 0) == first
        if along_x:
            return place(self.y, lax.rem(self.x + step, X_CHIPS), self.core)
        return place(lax.rem(self.y + step, Y_CHIPS), self.x, self.core)

    def block(self, half, step, item):
        if half == 0:
            return self.buf.at[lax.rem(self.y + step, Y_CHIPS), lax.rem(self.x + item, X_CHIPS), self.core, 0]
        return self.buf.at[lax.rem(self.y + item, Y_CHIPS), lax.rem(self.x + step, X_CHIPS), self.core, 1]

    def line(self, half, step, other=False):
        core = 1 - self.core if other else self.core
        if half == 0:
            return self.buf.at[lax.rem(self.y + step, Y_CHIPS), :, core, 0]
        return self.buf.at[:, lax.rem(self.x + step, X_CHIPS), core, 1]

    def spread(self, half, item):
        self.send.both_ways(
            self.block(half, 0, item),
            lambda i: self.s2.at[half, item, i],
            lambda i: self.r2.at[half, item, i],
            self.near(half, 1, False),
            self.near(half, 3, False),
        )

    def start(self, half):
        self.send.both_ways(
            self.block(half, 0, 0),
            lambda i: self.s1.at[half, i],
            lambda i: self.r1.at[half, i],
            self.near(half, 1, True),
            self.near(half, 3, True),
        )

    def relay(self, half):
        ref = self.block(half, 0, self.behind)
        arrived(ref, self.r1.at[half, self.core])
        to = self.near(half, self.ahead, True)
        self.send(ref, ref, self.s1.at[half, 2], self.r1.at[half, 2], to)
        self.spread(half, self.behind)

    def turn(self, half):
        arrived(self.block(half, 0, self.ahead), self.r1.at[half, 1 - self.core])
        self.spread(half, self.ahead)

    def turn_far(self, half):
        arrived(self.block(half, 0, 2), self.r1.at[half, 2])
        self.spread(half, 2)
        self.share(half, 0)

    def share(self, half, step):
        ref = self.line(half, step)
        to = place(self.y, self.x, 1 - self.core)
        self.send(ref, ref, self.sc.at[half, step], self.rc.at[half, step], to)

    def relay_line(self, half, item):
        ref = self.block(half, self.behind, item)
        arrived(ref, self.r2.at[half, item, self.core])
        to = self.near(half, self.ahead, False)
        self.send(ref, ref, self.s2.at[half, item, 2], self.r2.at[half, item, 2], to)

    def sides(self, half):
        for item in (0, self.behind, self.ahead, 2):
            arrived(self.block(half, self.ahead, item), self.r2.at[half, item, 1 - self.core])
        self.share(half, 3)
        self.share(half, 1)

    def far(self, half):
        for item in (0, self.behind, self.ahead, 2):
            arrived(self.block(half, 2, item), self.r2.at[half, item, 2])
        self.share(half, 2)

    def shared(self, half, step):
        arrived(self.line(half, step, other=True), self.rc.at[half, step])

    def begin(self):
        for step in (self.start, lambda half: self.spread(half, 0), self.relay, self.turn, self.turn_far):
            for half in range(2):
                step(half)

    def pass_on(self):
        for item in (0, self.behind, self.ahead, 2):
            for half in range(2):
                self.relay_line(half, item)


def layer_kernel(names, *refs):
    here = types.SimpleNamespace(**dict(zip(names, refs)))
    here.loaded = [name[:-4] for name in names if name[-4:] == "_any"]
    mix(here)
    experts(here)


def mix(ref):
    y, x, core = coordinates()
    ctx = lax.axis_index("ctx")
    devices = 2 * X_CHIPS * Y_CHIPS
    loaded = ref.loaded
    loads = {}
    for i, name in enumerate(loaded):
        loads[name] = pltpu.make_async_copy(getattr(ref, name + "_any"), getattr(ref, name), ref.load_sem.at[i])
        loads[name].start()
    ref.loads = loads
    segment, segments = lax.axis_index("segment"), lax.axis_size("segment")
    barrier = pltpu.get_barrier_semaphore()

    def hail(step, carry):
        peer = {"ctx": lax.rem(ctx + step, devices)}
        pl.semaphore_signal(barrier, inc=1, device_id=peer, device_id_type=pl.DeviceIdType.MESH)
        return carry

    lax.fori_loop(1, devices, hail, 0)
    for step in (1, segments - 1):
        peer = {"segment": lax.rem(segment + step, segments)}
        pl.semaphore_signal(barrier, inc=1, device_id=peer, device_id_type=pl.DeviceIdType.MESH)
    ref.kv_send = Sender()
    acts, gains, weights, kv = ref.acts, ref.gains, ref.weights, ref.kv
    normed, queries, first, mixed = ref.normed, ref.queries, ref.first, ref.mixed
    keep, drive, tail = ref.keep, ref.drive, ref.tail
    both, both_vmem = ref.both, ref.both_vmem
    second, packed, weighting = ref.second, ref.packed, ref.weighting
    rows, width = acts.shape
    lanes = 128
    blocks = width // lanes
    f32, bf16 = jnp.float32, jnp.bfloat16

    loads["w_kv"].wait()
    for half in range(2):
        weights[y, x, core, half] = ref.w_kv[half * 16 : half * 16 + 16]
    pl.semaphore_wait(barrier, devices + 1)
    w_gather = Gather(weights, [getattr(ref, "w_" + name) for name in GATHER_SEMS], Sender())
    w_gather.start(0)
    w_gather.start(1)
    w_gather.spread(0, 0)
    w_gather.spread(1, 0)
    for name in ("acts", "gains"):
        loads[name].wait()
    normed[...] = rms_norm(acts[...].astype(f32), gains[0]).astype(bf16)
    for step in (w_gather.relay, w_gather.turn, w_gather.turn_far):
        for half in range(2):
            step(half)
    for head in range(HEADS):
        group, place_in = divmod(head, HEADS // KVH)
        queries[group, place_in * rows : (place_in + 1) * rows] = normed[:, head * HD : (head + 1) * HD]
    w_gather.pass_on()
    for step in (w_gather.sides, w_gather.far):
        for half in range(2):
            step(half)
    for half in range(2):
        for step in (0, 3, 1, 2):
            w_gather.shared(half, step)

    for part in range(4):
        made = lax.dot_general(
            normed[...],
            weights[part].reshape(2 * HD, width),
            (((1,), (1,)), ((), ())),
            preferred_element_type=f32,
        ).astype(bf16)
        for head in range(2):
            kv[y, x, core, part % 2, part // 2 * 2 + head] = made[:, head * HD : (head + 1) * HD]

    kv_gather = Gather(kv, [getattr(ref, "kv_" + name) for name in GATHER_SEMS], ref.kv_send)
    kv_gather.begin()
    group = HEADS // KVH
    keys_here = 2 * X_CHIPS * rows
    queue = lax.broadcasted_iota(jnp.int32, (group, rows, 1), 1).reshape(group * rows, 1) + ctx * rows

    largest, total, summed = keep, drive, tail

    def of(g):
        return pl.ds(g * (group * rows // blocks), group * rows // blocks)

    def stacked(values):
        return values.reshape(group * rows // blocks, blocks, lanes)

    per_chip = 2 * rows
    on_chip = lax.broadcasted_iota(jnp.int32, (1, per_chip), 1)

    def attend_half(half, step):
        chips = []
        for item in range(4):
            down = lax.rem(y + step * (1 - half) + item * half, Y_CHIPS)
            along = lax.rem(x + step * half + item * (1 - half), X_CHIPS)
            chips.append((down, along))
        allowed = jnp.concatenate(
            [on_chip + (row * X_CHIPS + col) * per_chip <= queue for row, col in chips], 1
        )
        for head in range(2):
            g = 2 * half + head
            k, v = [
                jnp.concatenate(
                    [kv[row, col, :, half, i].reshape(per_chip, HD) for row, col in chips], 0
                )
                for i in (head, 2 + head)
            ]
            scores = lax.dot_general(
                queries[g], k, (((1,), (1,)), ((), ())), preferred_element_type=f32
            ) * (HD**-0.5 * LOG2E)
            scores = jnp.where(allowed, scores, -1e30)
            top = jnp.max(scores, -1, keepdims=True)
            if step == 0:
                newest = jnp.broadcast_to(top, (group * rows, lanes))
            else:
                oldest = largest[of(g)].reshape(group * rows, lanes)
                newest = jnp.maximum(oldest, top)
            wide = jnp.concatenate([newest] * (keys_here // lanes), 1)
            probs = jnp.exp2(scores - wide).astype(bf16)
            with_ones = jnp.concatenate([v, jnp.ones_like(v)], 1)
            made = jnp.dot(probs, with_ones, preferred_element_type=f32)
            weighed, sums = made[:, :HD], made[:, HD:]
            if step > 0:
                fade = jnp.exp2(oldest - newest)
                weighed = weighed + summed[of(g)].reshape(group * rows, lanes) * fade
                sums = sums + total[of(g)].reshape(group * rows, lanes) * fade
            summed[of(g)] = stacked(weighed)
            total[of(g)] = stacked(sums)
            largest[of(g)] = stacked(newest)

    def attend(step):
        for half in range(2):
            kv_gather.shared(half, step)

        def one_half(half, carry):
            attend_half(half, step)
            return carry

        lax.fori_loop(0, 2, one_half, 0)

    attend(0)
    kv_gather.pass_on()
    w_gather.send.finish()
    for half in range(2):
        kv_gather.sides(half)
    attend(3)
    for half in range(2):
        kv_gather.far(half)
    attend(1)
    attend(2)

    for g in range(KVH):
        made = (summed[of(g)] / total[of(g)]).reshape(group * rows, lanes)
        for r in range(group):
            span = slice((g * group + r) * HD, (g * group + r + 1) * HD)
            first[:, span] = acts[:, span].astype(f32) + made[r * rows : (r + 1) * rows]

    mixed[...] = rms_norm(first[...], gains[1]).astype(bf16)
    for name in loaded[3:-2]:
        loads[name].wait()
    transposed = (((1,), (1,)), ((), ()))
    both_vmem[:, 0:32] = lax.dot_general(
        mixed[...], ref.w_bc[...], transposed, preferred_element_type=f32
    )
    to_scalars = pltpu.make_async_copy(both_vmem, both, ref.load_sem.at[0])
    to_scalars.start()
    states = 16
    b_rows = lax.dot_general(
        ref.w_bc[0:states], mixed[...], transposed, preferred_element_type=f32
    )
    low_rank = jnp.dot(mixed[...], ref.dt_in[...], preferred_element_type=f32).astype(bf16)
    for i in range(blocks):
        span = slice(i * lanes, (i + 1) * lanes)
        raw = jnp.dot(low_rank, ref.dt_out[:, span], preferred_element_type=f32)
        raw = raw + ref.dt_bias[:, span]
        step_size = jnp.maximum(raw, 0.0) + jnp.log1p(jnp.exp(-jnp.abs(raw)))
        keep[:, i, :] = jnp.exp(-step_size * ref.decay_rate[:, span])
        drive[:, i, :] = step_size * mixed[:, span].astype(f32)

    def fade(turn, later):
        t = rows - 1 - turn
        tail[t] = drive[t] * later
        return later * keep[t]

    ref.product[...] = lax.fori_loop(0, rows, fade, jnp.ones((blocks, lanes), f32), unroll=4)

    def two_parts(value):
        high = value.astype(bf16)
        return high, (value - high.astype(f32)).astype(bf16)

    b_high, b_low = two_parts(b_rows)
    b_wide = jnp.concatenate([b_high, b_high, b_low], 1)
    message, inbox, outbox, incoming = ref.message, ref.inbox, ref.outbox, ref.incoming
    for i in range(blocks):
        high, low = two_parts(tail[:, i, :])
        ending = jnp.dot(b_wide, jnp.concatenate([high, low, high], 0), preferred_element_type=f32)
        for part in range(2):
            message[2 * i + part, 0] = ending[part * 8 : part * 8 + 8]
            message[2 * i + part, 1] = jnp.broadcast_to(ref.product[i : i + 1], (8, lanes))

    def swap(mine, theirs, semaphore):
        own = pltpu.make_async_copy(mine(ctx), theirs(ctx), ref.scan_recv.at[semaphore])
        own.start()

        def one(step, carry):
            peer = lax.rem(ctx + step, devices)
            pltpu.make_async_remote_copy(
                src_ref=mine(peer),
                dst_ref=theirs(ctx),
                send_sem=ref.scan_send.at[semaphore],
                recv_sem=ref.scan_recv.at[semaphore],
                device_id={"ctx": peer},
                device_id_type=pl.DeviceIdType.MESH,
            ).start()
            return carry

        lax.fori_loop(1, devices, one, 0)

    def advance(t, carry):
        state, product = carry
        kept, driven = keep[t], drive[t]
        moved, out = [], 0.0
        for n, old in enumerate(state):
            moved.append(old * kept + driven * both[t, n])
            out = out + moved[n] * both[t, states + n]
        product = product * kept
        drive[t] = out
        keep[t] = product
        return tuple(moved), product

    def join(turn, entering):
        outbox[turn] = entering
        return inbox[turn, 1] * entering + inbox[turn, 0]

    def slot(j):
        return incoming.at[
            pl.ds(pl.multiple_of(lax.rem(j, 2) * 8, 8), 8),
            pl.ds(pl.multiple_of(lax.div(j, 2) * lanes, lanes), lanes),
        ]

    swap(lambda j: message.at[j], lambda j: inbox.at[j], 0)
    to_scalars.wait()
    zero = jnp.zeros((blocks, lanes), f32)
    held = ((zero,) * states, jnp.ones((blocks, lanes), f32))
    held = lax.fori_loop(0, rows // 2, advance, held, unroll=4)
    arrived(inbox, ref.scan_recv.at[0])
    lax.fori_loop(0, devices, join, jnp.zeros((8, lanes), f32))
    swap(lambda j: outbox.at[j], slot, 1)
    lax.fori_loop(rows // 2, rows, advance, held, unroll=4)
    arrived(incoming, ref.scan_recv.at[1])
    c_high, c_low = two_parts(both_vmem[:, states : 2 * states])
    c_wide = jnp.concatenate([c_high, c_high, c_low], 1)
    for i in range(blocks):
        span = slice(i * lanes, (i + 1) * lanes)
        high, low = two_parts(incoming[:, span])
        carried = jnp.dot(c_wide, jnp.concatenate([high, low, high], 0), preferred_element_type=f32)
        second[:, span] = (
            first[:, span]
            + drive[:, i, :]
            + keep[:, i, :] * carried
            + ref.skip_gain[:, span] * mixed[:, span].astype(f32)
        )

    normed[...] = rms_norm(second[...], gains[2]).astype(bf16)
    logits = lax.dot_general(
        ref.w_router[...], normed[...], transposed, preferred_element_type=f32
    )
    expert = lax.broadcasted_iota(jnp.int32, (EXPERTS, rows), 0)
    hits = [(ref.routes[i : i + 1] == expert).astype(f32) for i in range(2)]
    chosen = [jnp.sum(hit * logits, 0, keepdims=True) for hit in hits]
    top = jnp.maximum(chosen[0], chosen[1])
    powers = [jnp.exp(c - top) for c in chosen]
    share = powers[0] + powers[1]
    gates = hits[0] * (powers[0] / share) + hits[1] * (powers[1] / share)
    hit = hits[0] + hits[1]
    row_at = lax.broadcasted_iota(jnp.int32, (rows, rows), 0)
    col_at = lax.broadcasted_iota(jnp.int32, (rows, rows), 1)
    earlier = (row_at < col_at).astype(bf16)
    rank = jnp.dot(hit.astype(bf16), earlier, preferred_element_type=f32)
    capacity = rows * 2 // EXPERTS
    slots = lax.broadcasted_iota(jnp.int32, (capacity, rows), 0).astype(f32)
    placing = []
    for e in range(EXPERTS):
        taken = (slots == rank[e : e + 1]).astype(f32) * hit[e : e + 1]
        weighting[e * capacity : (e + 1) * capacity] = taken * gates[e : e + 1]
        placing.append(taken.astype(bf16))
    placing = jnp.concatenate(placing, 0)
    for j in range(4):
        span = slice(j * width // 4, (j + 1) * width // 4)
        packed[:, :, :, :, span] = (
            jnp.dot(placing, normed[:, span], preferred_element_type=f32)
            .astype(bf16)
            .reshape(EXPERTS, 2, 2, 16, width // 4)
        )


def experts(ref):
    y, x, core = coordinates()
    left = lax.rem(x + X_CHIPS - 1, X_CHIPS)
    right = lax.rem(x + 1, X_CHIPS)
    far = lax.rem(x + 2, X_CHIPS)
    chips = (x, left, right, far)
    on_left, on_right, on_core = place(y, left, core), place(y, right, core), place(y, x, 1 - core)
    segments = lax.axis_size("segment")
    ahead = {"segment": lax.rem(lax.axis_index("segment") + 1, segments)}
    send, send_back, send_last = Sender(), Sender(), Sender()
    rows, parts, sibling_parts = ref.rows, ref.parts, ref.weights
    far_parts, side_parts, hidden, packed = ref.far_parts, ref.side_parts, ref.hidden, ref.packed
    out = ref.out
    f32, bf16 = jnp.float32, jnp.bfloat16
    capacity, width = far_parts.shape[1:]
    strip = width // 2
    strips = [pl.ds(j * strip, strip) for j in range(2)]

    def row_of(k):
        return lax.rem(y + k, Y_CHIPS)

    def block(at, k):
        return rows.at[chips[at], core, row_of(k)]

    def own_block(k):
        send(block(0, k), block(0, k), ref.send_side.at[0, k], ref.recv_side.at[0, k], on_right)
        send(block(0, k), block(0, k), ref.send_side.at[1, k], ref.recv_side.at[1, k], on_left)
        send(block(0, k), block(0, k), ref.send_core.at[0, k], ref.recv_core.at[0, k], on_core)

    def side_block(k):
        arrived(block(1, k), ref.recv_side.at[0, k])
        if k in (0, 1):
            send(block(1, k), block(1, k), ref.send_far.at[k], ref.recv_far.at[k], on_right)
        send(block(1, k), block(1, k), ref.send_core.at[1, k], ref.recv_core.at[1, k], on_core)
        arrived(block(2, k), ref.recv_side.at[1, k])
        if k in (2, 3):
            send(block(2, k), block(2, k), ref.send_far.at[k], ref.recv_far.at[k], on_left)
        send(block(2, k), block(2, k), ref.send_core.at[2, k], ref.recv_core.at[2, k], on_core)

    def far_block(k):
        arrived(block(3, k), ref.recv_far.at[k])
        send(block(3, k), block(3, k), ref.send_core.at[3, k], ref.recv_core.at[3, k], on_core)

    def from_core(at, steps):
        for k in steps:
            other = rows.at[chips[at], 1 - core, row_of(k)]
            arrived(other, ref.recv_core.at[at, k])

    def multiply(blocks):
        places = [(at, chips[at], row_of(k), k) for at, k in blocks]
        taken = [rows[chip, 1 - core, row].reshape(-1, width) for _, chip, row, _ in places]
        taken = taken + [rows[chip, core, row].reshape(-1, width) for _, chip, row, _ in places]
        count = len(places)
        used = slice(0, 2 * count * capacity)
        lifted = jnp.dot(jnp.concatenate(taken, 0), ref.up[...], preferred_element_type=f32)
        hidden[used] = jax.nn.silu(lifted).astype(bf16)
        for j, span in enumerate(strips):
            lowered = jnp.dot(hidden[used], ref.down[:, span], preferred_element_type=f32)
            lowered = lowered.astype(bf16).reshape(2 * count, capacity, strip)
            for i, (at, chip, row, k) in enumerate(places):
                rows[chip, 1 - core, row, :, :, :, span] = lowered[i].reshape(2, 2, 16, strip)
                parts[chip, row, :, span] = lowered[count + i]
                send_back(
                    rows.at[chip, 1 - core, row, :, :, :, span],
                    sibling_parts.at[chip, row, :, :, :, span],
                    ref.back_core_send.at[at, k, j],
                    ref.back_core_recv.at[at, k, j],
                    on_core,
                )

    thirds = [pl.ds(0, strip), pl.ds(strip, strip // 2), pl.ds(strip + strip // 2, strip // 2)]

    def mine(at, k, span):
        return parts.at[chips[at], row_of(k), :, span]

    def total(at, k, span, *more):
        theirs = sibling_parts[chips[at], row_of(k), :, :, :, span].reshape(capacity, span.size)
        made = mine(at, k, span)[...].astype(f32) + theirs.astype(f32)
        for slot in more:
            made = made + slot[...].astype(f32)
        return made.astype(bf16)

    def core_sum(at, k, j):
        ended = sibling_parts.at[chips[at], row_of(k), :, :, :, strips[j]]
        arrived(ended, ref.back_core_recv.at[at, k, j])

    def to_side(at, k, j):
        core_sum(at, k, j)
        mine(at, k, strips[j])[...] = total(at, k, strips[j])
        send_back(
            mine(at, k, strips[j]),
            side_parts.at[at - 1, k, :, strips[j]],
            ref.back_side_send.at[k, j],
            ref.back_side_recv.at[k, j],
            on_left if at == 1 else on_right,
        )

    def to_far(k, j):
        core_sum(3, k, j)
        mine(3, k, strips[j])[...] = total(3, k, strips[j])
        send_back(
            mine(3, k, strips[j]),
            far_parts.at[k, :, strips[j]],
            ref.back_far_send.at[k, j],
            ref.back_far_recv.at[k, j],
            on_left if k in (2, 1) else on_right,
        )

    def pass_on(k, j):
        at, span = 1 if k in (2, 1) else 2, thirds[j]
        if j < 2:
            core_sum(at, k, j)
            arrived(far_parts.at[k, :, strips[j]], ref.back_far_recv.at[k, j])
        mine(at, k, span)[...] = total(at, k, span, far_parts.at[k, :, span])
        send_last(
            mine(at, k, span),
            side_parts.at[at - 1, k, :, span],
            ref.back_relay_send.at[k, j],
            ref.back_relay_recv.at[k, j],
            on_left if at == 1 else on_right,
        )

    for k in (2, 1, 3):
        send(
            packed.at[row_of(k)],
            rows.at[x, core, y],
            ref.send_y.at[k],
            ref.recv_y.at[4 - k],
            place(row_of(k), x, core),
        )
    rows[x, core, y] = packed[y]
    own_block(0)
    for k in (2, 1, 3):
        arrived(block(0, k), ref.recv_y.at[k])
        own_block(k)
    count = 2 * X_CHIPS * Y_CHIPS - 1
    arrived(ref.inbox.at[pl.ds(0, count)], ref.scan_send.at[0])
    arrived(ref.outbox.at[pl.ds(0, count)], ref.scan_send.at[1])
    ref.kv_send.finish()
    side_block(0)
    ref.loads["up"].wait()
    ref.loads["down"].wait()
    early, late = (0, 2), (1, 3)
    from_core(0, early + late)
    multiply([(0, k) for k in early + late])
    side_block(2)
    for at in (1, 2):
        from_core(at, early)
    multiply([(at, k) for at in (1, 2) for k in early])
    for k in late:
        side_block(k)
    for at in (1, 2):
        from_core(at, late)
    multiply([(at, k) for at in (1, 2) for k in late])
    for k in early:
        far_block(k)
    for j in range(2):
        to_side(1, 0, j)
        to_side(2, 2, j)
    from_core(3, early)
    multiply([(3, k) for k in early])
    for k in late:
        far_block(k)
    for j in range(2):
        to_side(1, 3, j)
        to_side(2, 1, j)
    for j in range(2):
        for k in early:
            to_far(k, j)
    from_core(3, late)
    multiply([(3, k) for k in late])
    for j in range(2):
        for k in late:
            to_far(k, j)
    send.finish()
    order = (2, 0, 1, 3)
    for j in range(3):
        for k in order:
            pass_on(k, j)
    send_back.finish()
    gate = ref.weighting[...]
    high = gate.astype(bf16)
    low = (gate - high.astype(f32)).astype(bf16)
    over_slots = (((0,), (0,)), ((), ()))
    for j, span in enumerate(thirds):
        for k in order:
            relayed = 0 if k in (2, 1) else 1
            if j < 2:
                core_sum(0, k, j)
                arrived(side_parts.at[1 - relayed, k, :, strips[j]], ref.back_side_recv.at[k, j])
            arrived(side_parts.at[relayed, k, :, span], ref.back_relay_recv.at[k, j])
            made = total(0, k, span, side_parts.at[0, k, :, span], side_parts.at[1, k, :, span])
            if k == 0:
                out[y, :, span] = made
            else:
                mine(0, k, span)[...] = made
                send_last(
                    mine(0, k, span),
                    out.at[y, :, span],
                    ref.back_y_send.at[k, j],
                    ref.back_y_recv.at[4 - k, j],
                    place(row_of(k), x, core),
                )
        for k in (2, 1, 3):
            arrived(out.at[row_of(k), :, span], ref.back_y_recv.at[k, j])
        expert_out = out[:, :, span].reshape(-1, span.size)
        summed = lax.dot_general(high, expert_out, over_slots, preferred_element_type=f32)
        summed = summed + lax.dot_general(low, expert_out, over_slots, preferred_element_type=f32)
        ref.finished[:, span] = (ref.second[:, span] + summed).astype(bf16)
        send_last(
            ref.finished.at[:, span],
            ref.handed.at[:, span],
            ref.hand_send.at[j],
            ref.hand_recv.at[j],
            ahead,
        )
    for j, span in enumerate(thirds):
        arrived(ref.handed.at[:, span], ref.hand_recv.at[j])
    send_last.finish()


GATHER_SEMS = dict(s1=(2, 3), r1=(2, 3), s2=(2, 4, 3), r2=(2, 4, 3), sc=(2, 4), rc=(2, 4))


def layer(**given):
    rows, width = given["acts"].shape
    units = given["up"].shape[1]
    f32, bf16 = jnp.float32, jnp.bfloat16
    vmem = pltpu.VMEM
    capacity = rows * 2 // EXPERTS
    devices = 2 * X_CHIPS * Y_CHIPS
    blocks = width // 128
    grid = (Y_CHIPS, X_CHIPS, 2, 2)
    block = (capacity, width)
    scratch = {name: vmem(value.shape, value.dtype) for name, value in given.items()}
    scratch |= dict(
        weights=vmem(grid + (16, width), bf16),
        kv=vmem(grid + (4, rows, HD), bf16),
        normed=vmem((rows, width), bf16),
        queries=vmem((KVH, HEADS // KVH * rows, HD), bf16),
        first=vmem((rows, width), f32),
        mixed=vmem((rows, width), bf16),
        keep=vmem((rows, blocks, 128), f32),
        drive=vmem((rows, blocks, 128), f32),
        tail=vmem((rows, blocks, 128), f32),
        product=vmem((blocks, 128), f32),
        both_vmem=vmem((rows, 128), f32),
        both=pltpu.SMEM((rows, 128), f32),
        message=vmem((devices, 2, 8, 128), f32),
        inbox=vmem((devices, 2, 8, 128), f32),
        outbox=vmem((devices, 8, 128), f32),
        incoming=vmem((16, width), f32),
        second=vmem((rows, width), f32),
        packed=vmem((EXPERTS, 2, 2, 16, width), bf16),
        weighting=vmem((EXPERTS * capacity, rows), f32),
        rows=vmem((X_CHIPS, 2, Y_CHIPS, 2, 2, 16, width), bf16),
        parts=vmem((X_CHIPS, Y_CHIPS) + block, bf16),
        far_parts=vmem((Y_CHIPS,) + block, bf16),
        side_parts=vmem((2, Y_CHIPS) + block, bf16),
        hidden=vmem((2 * Y_CHIPS * capacity, units), bf16),
        out=vmem((EXPERTS,) + block, bf16),
        finished=vmem((rows, width), bf16),
    )
    sems = dict(
        load_sem=(len(given),),
        scan_send=(2,),
        scan_recv=(2,),
        send_y=(4,),
        recv_y=(4,),
        send_side=(2, 4),
        recv_side=(2, 4),
        send_far=(4,),
        recv_far=(4,),
        send_core=(4, 4),
        recv_core=(4, 4),
        back_core_send=(4, 4, 2),
        back_core_recv=(4, 4, 2),
        back_far_send=(4, 2),
        back_far_recv=(4, 2),
        back_side_send=(4, 2),
        back_side_recv=(4, 2),
        back_relay_send=(4, 3),
        back_relay_recv=(4, 3),
        back_y_send=(4, 3),
        back_y_recv=(4, 3),
        hand_send=(3,),
        hand_recv=(3,),
    )
    for gather in ("w_", "kv_"):
        sems |= {gather + name: shape for name, shape in GATHER_SEMS.items()}
    scratch |= {name: pltpu.SemaphoreType.DMA(shape) for name, shape in sems.items()}
    names = [name + "_any" for name in given] + ["handed"] + list(scratch)
    return pl.pallas_call(
        functools.partial(layer_kernel, names),
        out_shape=jax.ShapeDtypeStruct((rows, width), bf16),
        in_specs=[pl.BlockSpec(memory_space=pl.ANY)] * len(given),
        out_specs=pl.BlockSpec(memory_space=pltpu.VMEM),
        scratch_shapes=list(scratch.values()),
        compiler_params=pltpu.CompilerParams(
            collective_id=1, has_side_effects=True, vmem_limit_bytes=60 * MIB
        ),
        name="layer",
    )(*given.values())


def on_device(
    acts,
    norm_gains,
    w_kv,
    dt_in,
    dt_out,
    dt_bias,
    decay_rate,
    w_bc,
    skip_gain,
    w_router,
    routes,
    w_up,
    w_down,
):
    return layer(
        acts=acts[0],
        gains=norm_gains.transpose(1, 0, 2),
        w_kv=w_kv[0].T,
        dt_bias=dt_bias,
        decay_rate=decay_rate,
        skip_gain=skip_gain,
        routes=routes[0].T,
        dt_in=dt_in[0],
        dt_out=dt_out[0],
        w_bc=w_bc[0].T,
        w_router=w_router[0].T,
        up=w_up[0],
        down=w_down[0],
    )[None]


def solution(mesh):
    in_specs = (
        P("segment", "ctx", None),
        P("segment", None, None),
        P("segment", None, "ctx"),
        P("segment", None, None),
        P("segment", None, None),
        P("segment", None),
        P("segment", None),
        P("segment", None, None),
        P("segment", None),
        P("segment", None, None),
        P("segment", "ctx", None),
        P("segment", None, "ctx"),
        P("segment", "ctx", None),
    )
    out_specs = P("segment", "ctx", None)
    return jax.shard_map(
        on_device, mesh=mesh, in_specs=in_specs, out_specs=out_specs, check_vma=False
    )
```
